32 devices in a mesh: pipe: 4 (over z), ctx: 2 (over x), tp: 4 (over y, core).
Axes of the slice: x: 2, y: 2, z: 4, core: 2. Of those that a mesh axis runs over, the one named last changes fastest.
Arguments:
- inputs: bfloat16 [4, 512, 5120], P('pipe', ('ctx', 'tp')), may hold values from -6 to 6
- doc_lengths: int32 [4, 8], P('pipe'), may hold values from 1 to 256, 512 in all within a row
- w_query: bfloat16 [4, 5120, 3072], P('pipe', None, 'tp'), may hold values from -0.078125 to 0.078125
- w_key: bfloat16 [4, 5120, 1024], P('pipe', 'ctx', 'tp'), may hold values from -0.078125 to 0.078125
- w_value: bfloat16 [4, 5120, 1024], P('pipe', 'ctx', 'tp'), may hold values from -0.078125 to 0.078125
- w_out: bfloat16 [4, 3072, 5120], P('pipe', 'tp'), may hold values from -0.625 to 0.625
Outputs:
- next_input: bfloat16 [4, 512, 5120], P('pipe', ('ctx', 'tp'))
The draws below stay inside these ranges and needn't reach their ends.
Inputs may be any that keep to these rules, and one draw needn't show every extreme that they name: `doc_lengths`: the 8 lengths of a micro-batch sum to 512; the longest is exactly 256.
All inputs are finite; a program needn't handle non-finite values.
Results may differ from the reference program's by a relative error of at most 0.015.
Values may be sent and summed in bfloat16 or wider, within the bound.
No kernel may reach another device: no remote copies, remote signals or barrier semaphores. Data moves between devices by JAX's collectives and lax.ppermute only.
A program may use at most 64 MiB of HBM per device.

```python
import math
import jax
import jax.numpy as jnp
import numpy as np
from jax import lax

D = 5120
KH = 8
HD = 128
QH = 24
TOK_DEV = 256
SPAN = 1024
DOCS = 8
L = 512
SECTIONS = 4
N_TP = 4


def steps_of(own_key, shape, split, least, high):
    factor_of = 1.0
    for axis_at, blocks in split:
        steps = jax.random.uniform(jax.random.fold_in(jax.random.fold_in(own_key, 6), axis_at), (blocks,), jnp.float32, least / len(split), high / len(split))
        factor_of = factor_of * jnp.repeat(jnp.exp(steps), shape[axis_at] // blocks).reshape((-1,) + (1,) * (len(shape) - 1 - axis_at))
    return factor_of


def length_profile(count, total, bound, lean):
    weights = [(1 << 20) // math.isqrt(standing ** lean) + 1 for standing in range(2, count + 1)]
    surplus, given = total - bound - (count - 1), [1] * (count - 1)
    while surplus > 0:
        movable = [i for i in range(count - 1) if given[i] < bound]
        mass, budget = sum([weights[i] for i in movable]), surplus
        for i in movable:
            addition = min(bound - given[i], max(1, budget * weights[i] // mass), surplus)
            given[i] = given[i] + addition
            surplus = surplus - addition
    return np.array([bound] + given)


def uneven_parts(key, amount, total, limit, lean):
    if amount == 2:
        one = jax.random.randint(key, (), max(1, total - limit), min(limit, total - 1) + 1)
        return jnp.stack([one, total - one])
    sizes = jnp.asarray(length_profile(amount, total, limit, lean), jnp.int32)
    twos = (amount - 1) // 2
    source_of, receiver = sizes[1:1 + 2 * twos:2], sizes[2:2 + 2 * twos:2]
    margin = jnp.minimum(source_of - 1, limit - receiver)
    moved = jax.random.randint(jax.random.fold_in(key, 1), (twos,), 0, 1 << 20) % (margin + 1)
    sizes = sizes.at[1:1 + 2 * twos:2].set(source_of - moved).at[2:2 + 2 * twos:2].set(receiver + moved)
    return sizes[jax.random.permutation(jax.random.fold_in(key, 2), amount)]


def noise(rng, dims, width, limit, shards=(), kind=jnp.bfloat16):
    values = width * jax.random.normal(rng, dims, jnp.float32)
    if shards:
        values = values * steps_of(rng, dims, shards, -0.22, 0.18)
    return jnp.clip(values, -limit, limit).astype(kind)


def setup_inputs(seed: int = 0) -> dict:
    arg_keys = jax.random.split(jax.random.key(seed), 7)
    inputs = noise(arg_keys[0], (SECTIONS, L, D), 1.0, 6.0, ((0, 4), (1, 8)))
    doc_lengths = jax.vmap(lambda own: uneven_parts(own, DOCS, L, L // 2, 2))(jax.random.split(arg_keys[1], SECTIONS)).reshape((SECTIONS, DOCS)).astype(jnp.int32)
    w_query = noise(arg_keys[2], (SECTIONS, D, QH * HD), D ** -0.5, 0.078125, ((0, 4), (2, 4)))
    w_key = noise(arg_keys[3], (SECTIONS, D, KH * HD), D ** -0.5, 0.078125, ((0, 4), (1, 2), (2, 4)))
    w_value = noise(arg_keys[4], (SECTIONS, D, KH * HD), D ** -0.5, 0.078125, ((0, 4), (1, 2), (2, 4)))
    w_out = noise(arg_keys[5], (SECTIONS, QH * HD, D), (QH * HD // 32) ** -0.5, 0.625, ((0, 4), (1, 4)))
    return dict(inputs=inputs, doc_lengths=doc_lengths, w_query=w_query, w_key=w_key, w_value=w_value, w_out=w_out)


ROPE_BASE = 500000.0
NORM_EPS = 1e-06

def doc_index(positions, lengths):
    doc_ends = jnp.cumsum(lengths)
    return lax.optimization_barrier(jnp.sum((positions[:, None] >= doc_ends[None, :]).astype(jnp.int32), axis=1))

def norm_rotate(entries, positions, head_count, head_width):
    row_count = entries.shape[0]
    shaped = entries.reshape(row_count, head_count, head_width)
    shaped = shaped * lax.rsqrt(lax.optimization_barrier(jnp.mean(shaped * shaped, axis=-1, keepdims=True)) + NORM_EPS)
    half_width = head_width // 2
    frequencies = jnp.power(ROPE_BASE, -(jnp.arange(half_width, dtype=jnp.float32) * 2.0 / head_width))
    angles = positions.astype(jnp.float32)[:, None] * frequencies[None, :]
    cosine = jnp.cos(angles)[:, None, :]
    sine_part = jnp.sin(angles)[:, None, :]
    first_half = shaped[..., :half_width]
    second = shaped[..., half_width:]
    turned = jnp.concatenate([first_half * cosine - second * sine_part, second * cosine + first_half * sine_part], axis=-1)
    return turned.reshape(row_count, head_count * head_width)

def layer_forward(inputs, lengths, w_query, w_key, w_value, w_out):
    seq_len = inputs.shape[0]
    group_size = QH // KH
    positions = jnp.arange(seq_len, dtype=jnp.int32)
    docs = doc_index(positions, lengths)
    queries = jnp.dot(inputs, w_query, preferred_element_type=jnp.float32)
    key_rows = jnp.dot(inputs, w_key, preferred_element_type=jnp.float32)
    value_rows = jnp.dot(inputs, w_value, preferred_element_type=jnp.float32)
    q_round = norm_rotate(queries, positions, QH, HD).astype(jnp.bfloat16).reshape(seq_len, KH, group_size, HD)
    k_round = norm_rotate(key_rows, positions, KH, HD).astype(jnp.bfloat16).reshape(seq_len, KH, HD)
    v_round = value_rows.astype(jnp.bfloat16).reshape(seq_len, KH, HD)
    k_float = k_round.astype(jnp.float32)
    v_float = v_round.astype(jnp.float32)
    score_scale = 1.0 / HD ** 0.5

    def one_block(start_row):
        q_part = lax.dynamic_slice_in_dim(q_round, start_row, TOK_DEV, 0).astype(jnp.float32)
        q_pos = lax.dynamic_slice_in_dim(positions, start_row, TOK_DEV, 0)
        q_doc = lax.dynamic_slice_in_dim(docs, start_row, TOK_DEV, 0)
        scores = jnp.einsum('tkgd,nkd->kgtn', q_part, k_float) * score_scale
        allowed = (positions[None, :] <= q_pos[:, None]) & (docs[None, :] == q_doc[:, None]) & (positions[None, :] // SPAN == q_pos[:, None] // SPAN)
        weights = lax.optimization_barrier(jnp.where(allowed[None, None], jnp.exp(scores), 0.0).astype(jnp.bfloat16))
        weights = weights.astype(jnp.float32)
        numerator = jnp.einsum('kgtn,nkd->tkgd', weights, v_float)
        denominator = lax.optimization_barrier(jnp.sum(weights, axis=-1))
        return (numerator / jnp.transpose(denominator, (2, 0, 1))[..., None]).astype(jnp.bfloat16)
    starts = jnp.arange(seq_len // TOK_DEV, dtype=jnp.int32) * TOK_DEV
    attended = lax.map(one_block, starts).reshape(seq_len, QH * HD)
    share = QH * HD // N_TP

    def add_group(total, group_index):
        attended_part = lax.dynamic_slice_in_dim(attended, group_index * share, share, 1)
        weight_part = lax.dynamic_slice_in_dim(w_out, group_index * share, share, 0)
        product = lax.optimization_barrier(jnp.dot(attended_part, weight_part, preferred_element_type=jnp.float32).astype(jnp.bfloat16))
        return (total + product.astype(jnp.float32), group_index)
    mixed, unused = lax.scan(add_group, jnp.zeros((seq_len, inputs.shape[1]), jnp.float32), jnp.arange(N_TP, dtype=jnp.int32))
    return mixed.astype(jnp.bfloat16)

def section_forward(packed):
    return layer_forward(packed[0], packed[1], packed[2], packed[3], packed[4], packed[5])

def reference(inputs, doc_lengths, w_query, w_key, w_value, w_out):
    outputs = lax.map(section_forward, (inputs, doc_lengths, w_query, w_key, w_value, w_out))
    return jnp.roll(outputs, 1, axis=0)
```

```python
import functools

import jax
import jax.numpy as jnp
from jax import lax
from jax.experimental import pallas as pl
from jax.experimental.pallas import tpu as pltpu
from jax.sharding import PartitionSpec as P

HD = 128
SPAN = 1024
ROPE_BASE = 500000.0
NORM_EPS = 1e-06
OUT_CHUNKS = 4
MIB = 1 << 20


def from_behind(value, axis, steps):
    count = lax.axis_size(axis)
    pairs = [(source, (source + steps) % count) for source in range(count)]
    return lax.ppermute(value, axis, pairs)


def swap(value, axis, bit):
    count = lax.axis_size(axis)
    return lax.ppermute(value, axis, [(source, source ^ bit) for source in range(count)])


def rope_tables(positions):
    half_width = HD // 2
    frequencies = jnp.power(ROPE_BASE, -(jnp.arange(half_width, dtype=jnp.float32) * 2.0 / HD))
    angles = positions.astype(jnp.float32)[:, None] * frequencies[None, :]
    cosine, sine = jnp.cos(angles), jnp.sin(angles)
    return jnp.concatenate([cosine, cosine], 1), jnp.concatenate([-sine, sine], 1)


def norm_rotate_head(head, cosine, sine):
    head = head * lax.rsqrt(jnp.mean(head * head, axis=-1, keepdims=True) + NORM_EPS)
    return head * cosine + pltpu.roll(head, HD // 2, 1) * sine


def call(kernel, out_shape, mib, flops, moved, **given):
    return pl.pallas_call(
        kernel,
        out_shape=out_shape,
        compiler_params=pltpu.CompilerParams(vmem_limit_bytes=mib * MIB),
        cost_estimate=pl.CostEstimate(flops=flops, bytes_accessed=moved, transcendentals=0),
        **given,
    )


def shape(rows, columns, dtype):
    return jax.ShapeDtypeStruct((rows, columns), dtype)


def project_kernel(x_count, w_count, widths, *refs):
    xs, ws = refs[:x_count], refs[x_count : x_count + w_count]
    outs, acc = refs[x_count + w_count : -1], refs[-1]
    step = pl.program_id(0)

    @pl.when(step == 0)
    def _():
        acc[...] = jnp.zeros_like(acc)

    rows = jnp.concatenate([x[...] for x in xs], axis=0) if x_count > 1 else xs[0][...]
    at = 0
    for w in ws:
        wide = w.shape[1]
        acc[:, at : at + wide] += jnp.dot(rows, w[...], preferred_element_type=jnp.float32)
        at += wide

    @pl.when(step == pl.num_programs(0) - 1)
    def _():
        for out, (first, last) in zip(outs, widths):
            out[...] = acc[first:last, :].astype(out.dtype)


def project_kv(xs, ws, outs):
    rows, depth = xs[0].shape
    block = 512
    wide = sum(w.shape[1] for w in ws)
    count = len(xs)
    return call(
        functools.partial(project_kernel, count, len(ws), [(a, b) for a, b, _ in outs]),
        [shape(b - a, wide, dtype) for a, b, dtype in outs],
        16,
        2 * count * rows * depth * wide,
        2 * depth * wide + 2 * count * rows * depth,
        grid=(depth // block,),
        in_specs=[pl.BlockSpec((rows, block), lambda i: (0, i))] * count
        + [pl.BlockSpec((block, w.shape[1]), lambda i: (i, 0)) for w in ws],
        out_specs=[pl.BlockSpec((b - a, wide), lambda i: (0, 0)) for a, b, _ in outs],
        scratch_shapes=[pltpu.VMEM((count * rows, wide), jnp.float32)],
    )(*xs, *ws)


def query_first_kernel(half_ref, x0, x1, w0, w1, out):
    @pl.when(pl.program_id(0) == 0)
    def _():
        out[...] = jnp.zeros_like(out)

    rows = jnp.concatenate([x0[...], x1[...]], axis=0)
    wide = w0.shape[1]
    out[:, :wide] += jnp.dot(rows, w0[...], preferred_element_type=jnp.float32)
    out[:, wide:] += jnp.dot(rows, w1[...], preferred_element_type=jnp.float32)


def query_last_kernel(half_ref, x0, x1, w0, w1, before, cosine, sine, out, acc):
    @pl.when(pl.program_id(0) == 0)
    def _():
        acc[...] = before[...]

    rows = jnp.concatenate([x0[...], x1[...]], axis=0)
    wide = w0.shape[1]
    acc[:, :wide] += jnp.dot(rows, w0[...], preferred_element_type=jnp.float32)
    acc[:, wide:] += jnp.dot(rows, w1[...], preferred_element_type=jnp.float32)

    @pl.when(pl.program_id(0) == pl.num_programs(0) - 1)
    def _():
        for at in range(0, acc.shape[1], HD):
            turned = norm_rotate_head(acc[:, at : at + HD], cosine[...], sine[...])
            out[:, at : at + HD] = turned.astype(out.dtype)


def project_query(half, x0, x1, w0, w1, before=None, tables=None):
    rows, depth = x0.shape
    wide = w0.shape[1]
    block = 512
    steps = depth // block
    in_specs = [
        pl.BlockSpec((rows, block), lambda i, h: (0, i)),
        pl.BlockSpec((rows, block), lambda i, h: (0, i)),
        pl.BlockSpec((block, wide), lambda i, h: (h[0] * steps + i, 0)),
        pl.BlockSpec((block, wide), lambda i, h: (h[0] * steps + i, 0)),
    ]
    arguments = [half, x0, x1, w0, w1]
    whole = lambda *dims: pl.BlockSpec(dims, lambda i, h: (0, 0))
    if before is None:
        kernel, dtype, scratch = query_first_kernel, jnp.float32, []
    else:
        kernel, dtype = query_last_kernel, jnp.bfloat16
        scratch = [pltpu.VMEM((2 * rows, 2 * wide), jnp.float32)]
        in_specs += [whole(2 * rows, 2 * wide), whole(2 * rows, HD), whole(2 * rows, HD)]
        arguments += [before, *tables]
    return call(
        kernel,
        shape(2 * rows, 2 * wide, dtype),
        20,
        8 * rows * depth * wide,
        4 * depth * wide + 4 * rows * depth,
        grid_spec=pltpu.PrefetchScalarGridSpec(
            num_scalar_prefetch=1,
            grid=(steps,),
            in_specs=in_specs,
            out_specs=whole(2 * rows, 2 * wide),
            scratch_shapes=scratch,
        ),
    )(*arguments)


def finish_kernel(own, own_a, own_b, far_a, far_b, early, cosine, sine, out):
    piece = own_a.shape[0]
    rows = 2 * piece
    keys = own.shape[1] // 2
    for at in range(0, 4 * piece, piece):
        part = pl.ds(at % rows, piece)
        if at < rows:
            total = early[part, :].astype(jnp.float32)
            total = total + (far_a, far_b)[at // piece][...].astype(jnp.float32)
        else:
            total = own[part, :] + (own_a, own_b)[at // piece - 2][...].astype(jnp.float32)
        turn = pl.ds(at, piece)
        for head in range(0, keys, HD):
            key = norm_rotate_head(total[:, head : head + HD], cosine[turn, :], sine[turn, :])
            out[turn, head : head + HD] = key.astype(out.dtype)
        out[turn, keys:] = total[:, keys:].astype(out.dtype)


def attend_kernel(group, q, mine, other, first, last, k_pos, out):
    rows = q.shape[0]
    keys = mine.shape[1] // 2
    heads = keys // HD
    allowed = (k_pos[...] >= first[...]) & (k_pos[...] <= last[...])
    allowed = jnp.concatenate([allowed.astype(jnp.float32)] * group, axis=0) > 0.5
    for head in range(heads):
        here, there = head * HD, (head + heads // 2) % heads * HD
        key = jnp.concatenate([mine[:, here : here + HD], other[:, there : there + HD]], 0)
        here, there = here + keys, there + keys
        value = jnp.concatenate([mine[:, here : here + HD], other[:, there : there + HD]], 0)
        at = head * group * HD
        query = jnp.concatenate([q[:, at + g * HD : at + (g + 1) * HD] for g in range(group)], 0)
        scores = lax.dot_general(
            query, key, (((1,), (1,)), ((), ())), preferred_element_type=jnp.float32
        )
        weights = jnp.where(allowed, jnp.exp(scores * (1.0 / HD**0.5)), 0.0)
        weights = weights.astype(jnp.bfloat16)
        total = jnp.sum(weights.astype(jnp.float32), axis=-1, keepdims=True)
        mixed = jnp.dot(weights, value, preferred_element_type=jnp.float32) / total
        mixed = mixed.astype(out.dtype)
        for g in range(group):
            out[:, at + g * HD : at + (g + 1) * HD] = mixed[g * rows : (g + 1) * rows, :]


def out_kernel(attended, w0, w1, stay, leave):
    depth = w0.shape[0]
    total = jnp.dot(attended[:, :depth], w0[...], preferred_element_type=jnp.float32)
    total += jnp.dot(attended[:, depth:], w1[...], preferred_element_type=jnp.float32)
    half = stay.shape[0]
    stay[...] = total[:half]
    leave[...] = total[half:].astype(leave.dtype)


def project_out(attended, w0, w1, chunk):
    rows = attended.shape[0]
    depth, wide = w0.shape
    block = 256
    steps = wide // OUT_CHUNKS // block
    first = chunk * steps
    return call(
        out_kernel,
        [
            shape(rows // 2, steps * block, jnp.float32),
            shape(rows // 2, steps * block, jnp.bfloat16),
        ],
        8,
        4 * rows * depth * steps * block,
        4 * depth * steps * block,
        grid=(steps,),
        in_specs=[
            pl.BlockSpec((rows, 2 * depth), lambda i: (0, 0)),
            pl.BlockSpec((depth, block), lambda i: (0, first + i)),
            pl.BlockSpec((depth, block), lambda i: (0, first + i)),
        ],
        out_specs=[
            pl.BlockSpec((rows // 2, block), lambda i: (0, i)),
            pl.BlockSpec((rows // 2, block), lambda i: (0, i)),
        ],
    )(attended, w0, w1)


def on_four_by_two(inputs, doc_lengths, w_query, w_key, w_value, w_out):
    own = inputs[0]
    w_query, w_key, w_value, w_out = w_query[0], w_key[0], w_value[0], w_out[0]
    rows = own.shape[0]
    half = w_key.shape[0]
    group = w_query.shape[1] // w_key.shape[1]
    ctx, tp = lax.axis_index("ctx"), lax.axis_index("tp")
    block_rows = rows * lax.axis_size("tp")

    x_far = lax.dynamic_slice_in_dim(own, (1 - ctx) * half, half, 1)
    x_near = lax.dynamic_slice_in_dim(own, ctx * half, half, 1)
    far_a = swap(x_far, "ctx", 1)
    near_b = swap(x_near, "tp", 2)
    key_s = swap(w_key, "tp", 1)
    value_s = swap(w_value, "tp", 1)
    query_s = swap(w_query, "tp", 1)
    out_s = swap(w_out, "tp", 1)
    far_b = swap(far_a, "tp", 2)

    piece = jnp.arange(rows, dtype=jnp.int32)
    base = ctx * block_rows
    here = jnp.concatenate([piece + rows * tp, piece + rows * (tp ^ 2)]) + base
    there = jnp.concatenate([piece + rows * (tp ^ 1), piece + rows * (tp ^ 3)]) + base
    k_pos = jnp.concatenate([here - block_rows, here, there - block_rows, there])[None, :]
    ends = jnp.cumsum(doc_lengths[0])
    doc_start = jnp.max(jnp.where(ends[None, :] <= here[:, None], ends[None, :], 0), axis=1)
    first = jnp.maximum(doc_start, here // SPAN * SPAN)[:, None]
    cosine, sine = rope_tables(jnp.concatenate([here - block_rows, here]))

    weights = [w_key, key_s, w_value, value_s]
    own_sum, own_send, far_sum_a = project_kv(
        [x_near, near_b, far_a],
        weights,
        [
            (0, 2 * rows, jnp.float32),
            (0, 2 * rows, jnp.bfloat16),
            (2 * rows, 3 * rows, jnp.bfloat16),
        ],
    )
    early = lax.ppermute(own_send, "ctx", [(0, 1)])
    own_a = swap(far_sum_a, "ctx", 1)
    far_sum_b = project_kv([far_b], weights, [(0, rows, jnp.bfloat16)])[0]
    own_b = swap(far_sum_b, "ctx", 1)
    far_c = swap(x_far, "tp", 2)

    near = jnp.reshape(ctx, (1,))
    queries = project_query(near, x_near, near_b, w_query, query_s)
    queries = project_query(
        1 - near, x_far, far_c, w_query, query_s, queries, (cosine[2 * rows :], sine[2 * rows :])
    )

    kv_shape = shape(4 * rows, own_sum.shape[1], jnp.bfloat16)
    kv_mine = call(finish_kernel, kv_shape, 8, 0, 1 << 20)(
        own_sum, own_a, own_b, far_sum_a, far_sum_b, early, cosine, sine
    )
    kv_other = swap(kv_mine, "tp", 1)
    attended = call(
        functools.partial(attend_kernel, group),
        shape(2 * rows, queries.shape[1], jnp.bfloat16),
        16,
        8 * rows * 8 * rows * queries.shape[1],
        1 << 20,
    )(queries, kv_mine, kv_other, first, here[:, None], k_pos)

    parts = []
    for chunk in range(OUT_CHUNKS):
        stay, leave = project_out(attended, w_out, out_s, chunk)
        arrived = swap(leave, "tp", 2)
        mixed = (stay + arrived.astype(jnp.float32)).astype(jnp.bfloat16)
        parts.append(from_behind(mixed, "pipe", 1))
    return jnp.concatenate(parts, axis=1)[None]


def doc_index(positions, lengths):
    doc_ends = jnp.cumsum(lengths)
    return jnp.sum((positions[:, None] >= doc_ends[None, :]).astype(jnp.int32), axis=1)


def norm_rotate(entries, positions, head_count, head_width):
    row_count = entries.shape[0]
    shaped = entries.reshape(row_count, head_count, head_width)
    shaped = shaped * lax.rsqrt(jnp.mean(shaped * shaped, axis=-1, keepdims=True) + NORM_EPS)
    half_width = head_width // 2
    frequencies = jnp.power(
        ROPE_BASE, -(jnp.arange(half_width, dtype=jnp.float32) * 2.0 / head_width)
    )
    angles = positions.astype(jnp.float32)[:, None] * frequencies[None, :]
    cosine = jnp.cos(angles)[:, None, :]
    sine_part = jnp.sin(angles)[:, None, :]
    first_half = shaped[..., :half_width]
    second = shaped[..., half_width:]
    turned = jnp.concatenate(
        [first_half * cosine - second * sine_part, second * cosine + first_half * sine_part],
        axis=-1,
    )
    return turned.reshape(row_count, head_count * head_width)


def attend(queries, q_pos, q_doc, key_rows, value_rows, k_pos, k_doc):
    score_scale = 1.0 / HD**0.5
    scores = (
        jnp.einsum("tkgd,nkd->kgtn", queries, key_rows, preferred_element_type=jnp.float32)
        * score_scale
    )
    allowed = (
        (k_pos[None, :] <= q_pos[:, None])
        & (k_doc[None, :] == q_doc[:, None])
        & (k_pos[None, :] // SPAN == q_pos[:, None] // SPAN)
    )
    weights = jnp.where(allowed[None, None], jnp.exp(scores), 0.0).astype(jnp.bfloat16)
    numerator = jnp.einsum(
        "kgtn,nkd->tkgd", weights, value_rows, preferred_element_type=jnp.float32
    )
    denominator = jnp.sum(weights.astype(jnp.float32), axis=-1)
    return (numerator, denominator)


def on_any(inputs, doc_lengths, w_query, w_key, w_value, w_out):
    tok_rows = lax.all_gather(inputs[0], "tp", axis=0, tiled=True)
    block_rows = tok_rows.shape[0]
    q_heads = w_query.shape[2] // HD
    kv_heads = w_key.shape[2] // HD
    group_size = q_heads // kv_heads
    ctx_rank = lax.axis_index("ctx")
    positions = ctx_rank * block_rows + jnp.arange(block_rows, dtype=jnp.int32)
    lengths = doc_lengths[0]
    own_docs = doc_index(positions, lengths)
    queries = jnp.dot(tok_rows, w_query[0], preferred_element_type=jnp.float32)
    stacked_weights = jnp.stack([w_key[0], w_value[0]])
    key_value = jnp.einsum(
        "td,sdc->stc",
        tok_rows,
        lax.all_gather(stacked_weights, "ctx", axis=1, tiled=True),
        preferred_element_type=jnp.float32,
    )
    keys_float = key_value[0]
    values_float = key_value[1]
    q_round = (
        norm_rotate(queries, positions, q_heads, HD)
        .astype(jnp.bfloat16)
        .reshape(block_rows, kv_heads, group_size, HD)
    )
    k_round = norm_rotate(keys_float, positions, kv_heads, HD).astype(jnp.bfloat16)
    v_round = values_float.astype(jnp.bfloat16)
    key_value_pair = jnp.stack([k_round, v_round])
    shard_piece = lax.all_gather(key_value_pair, "ctx", axis=1, tiled=True)
    row_count = shard_piece.shape[1]
    k_pos = jnp.arange(row_count, dtype=jnp.int32)
    k_doc = doc_index(k_pos, lengths)
    key_rows = shard_piece[0].reshape(row_count, kv_heads, HD)
    value_rows = shard_piece[1].reshape(row_count, kv_heads, HD)
    numerator, denominator = attend(
        q_round, positions, own_docs, key_rows, value_rows, k_pos, k_doc
    )
    attended = (
        (numerator / jnp.transpose(denominator, (2, 0, 1))[..., None])
        .astype(jnp.bfloat16)
        .reshape(block_rows, q_heads * HD)
    )
    mixed = lax.psum_scatter(
        jnp.dot(attended, w_out[0], preferred_element_type=jnp.float32).astype(jnp.bfloat16),
        "tp",
        scatter_dimension=0,
        tiled=True,
    )
    return from_behind(mixed, "pipe", 1)[None]


def solution(mesh):
    in_specs = (
        P("pipe", ("ctx", "tp"), None),
        P("pipe", None),
        P("pipe", None, "tp"),
        P("pipe", "ctx", "tp"),
        P("pipe", "ctx", "tp"),
        P("pipe", "tp", None),
    )
    out_specs = P("pipe", ("ctx", "tp"), None)
    paired = mesh.shape["ctx"] == 2 and mesh.shape["tp"] == 4
    return jax.shard_map(
        on_four_by_two if paired else on_any,
        mesh=mesh,
        in_specs=in_specs,
        out_specs=out_specs,
        check_vma=False,
    )
```

```python
import functools
import math

import jax
import jax.numpy as jnp
from jax import lax
from jax.experimental import pallas as pl
from jax.experimental.pallas import tpu as pltpu
from jax.sharding import PartitionSpec as P

HD = 128
SPAN = 1024
ROPE_BASE = 500000.0
NORM_EPS = 1e-06
OUT_CHUNKS = 4
MIB = 1 << 20


def from_behind(value, axis, steps):
    count = lax.axis_size(axis)
    pairs = [(source, (source + steps) % count) for source in range(count)]
    return lax.ppermute(value, axis, pairs)


def swap(value, axis, bit):
    count = lax.axis_size(axis)
    return lax.ppermute(value, axis, [(source, source ^ bit) for source in range(count)])


def norm_rotate_head(head, cosine, sine):
    head = head * lax.rsqrt(jnp.mean(head * head, axis=-1, keepdims=True) + NORM_EPS)
    return head * cosine + pltpu.roll(head, HD // 2, 1) * sine


def shape(rows, columns, dtype):
    return jax.ShapeDtypeStruct((rows, columns), dtype)


def in_vmem(value):
    return pltpu.with_memory_space_constraint(value, pltpu.VMEM)


def call(kernel, out_shape, mib, flops, moved, **given):
    return pl.pallas_call(
        kernel,
        out_shape=out_shape,
        compiler_params=pltpu.CompilerParams(vmem_limit_bytes=mib * MIB),
        cost_estimate=pl.CostEstimate(flops=flops, bytes_accessed=moved, transcendentals=0),
        **given,
    )


def after(value, *others):
    return lax.optimization_barrier((value, *others))[0]


def piece_positions(start, index, rows, pieces, dims, axis):
    at = lax.broadcasted_iota(jnp.int32, dims, axis)
    positions = at % rows + start
    for order, (shift, flip) in enumerate(pieces):
        offset = shift + rows * (index ^ flip)
        positions = positions + jnp.where(at // rows == order, offset, 0)
    return positions


def tables_kernel(rows, block_rows, place, lengths, cosine, sine, allowed):
    start, index = place[0] * block_rows, place[1]
    keys = [(shift, flip) for shift in (-block_rows, 0) for flip in range(4)]
    dims = cosine.shape
    positions = piece_positions(start, index, rows, keys, dims, 0).astype(jnp.float32)
    lane = lax.broadcasted_iota(jnp.int32, dims, 1)
    power = (lane % (HD // 2)).astype(jnp.float32) * (2.0 / HD)
    angles = positions * jnp.exp(power * -math.log(ROPE_BASE))
    cosine[...] = jnp.cos(angles)
    sine[...] = jnp.sin(angles) * jnp.where(lane < HD // 2, -1.0, 1.0)
    dims = allowed.shape
    q_pos = piece_positions(start, index, rows, [(0, flip) for flip in (0, 2, 1, 3)], dims, 0)
    k_pos = piece_positions(start, index, rows, keys, dims, 1)
    first = q_pos // SPAN * SPAN
    end = 0
    for doc in range(lengths.shape[1]):
        end = end + lengths[0, doc]
        first = jnp.where(end <= q_pos, jnp.maximum(first, end), first)
    allowed[...] = jnp.where((k_pos >= first) & (k_pos <= q_pos), 1.0, 0.0)


def stacked(pieces):
    return jnp.concatenate([piece[...] for piece in pieces], axis=0)


def project_kernel(x_count, w_count, ranges, *refs):
    xs, ws, outs = refs[:x_count], refs[x_count : x_count + w_count], refs[x_count + w_count :]
    rows = stacked(xs)
    at = 0
    for w in ws:
        wide = w.shape[1]
        total = jnp.dot(rows, w[...], preferred_element_type=jnp.float32)
        for out, (first, last) in zip(outs, ranges):
            out[:, at : at + wide] = total[first:last, :].astype(out.dtype)
        at += wide


def project_kv(xs, ws, outs):
    rows, depth = xs[0].shape
    wide = sum(w.shape[1] for w in ws)
    count = len(xs)
    return call(
        functools.partial(project_kernel, count, len(ws), [(a, b) for a, b, _ in outs]),
        [shape(b - a, wide, dtype) for a, b, dtype in outs],
        8,
        2 * count * rows * depth * wide,
        2 * count * rows * depth,
    )(*xs, *ws)


def query_kernel(x_count, last, half, *refs):
    xs, w = refs[:x_count], refs[x_count]
    rows = stacked(xs)
    depth = rows.shape[1]
    block = 2 * HD
    part = pl.ds(pl.multiple_of(half[0] * depth, depth), depth)
    if last:
        before, cosine, sine, out = refs[x_count + 1 :]
        piece, whole = xs[0].shape[0], rows.shape[0]
        order = [pl.ds(whole + piece * flip, piece) for flip in (0, 2, 1, 3)]
        cosine = jnp.concatenate([cosine[at, :] for at in order], axis=0)
        sine = jnp.concatenate([sine[at, :] for at in order], axis=0)
    else:
        out = refs[x_count + 1]
    for at in range(0, w.shape[1], block):
        total = jnp.dot(rows, w[part, at : at + block], preferred_element_type=jnp.float32)
        if last:
            total = total + before[:, at : at + block]
            for head in range(0, block, HD):
                query = norm_rotate_head(total[:, head : head + HD], cosine, sine)
                out[:, at + head : at + head + HD] = query.astype(out.dtype)
        else:
            out[:, at : at + block] = total


def project_query(half, xs, w, *rest):
    rows, depth = xs[0].shape
    rows = rows * len(xs)
    wide = w.shape[1]
    return call(
        functools.partial(query_kernel, len(xs), bool(rest)),
        shape(rows, wide, jnp.bfloat16 if rest else jnp.float32),
        16,
        2 * rows * depth * wide,
        4 * rows * depth,
        in_specs=[pl.BlockSpec(memory_space=pltpu.SMEM)]
        + [pl.BlockSpec(memory_space=pltpu.VMEM)] * (len(xs) + 1 + len(rest)),
    )(half, *xs, w, *rest)


def finish(total, cosine, sine, out, at):
    rows, wide = total.shape
    keys = wide // 2
    part = pl.ds(at, rows)
    for head in range(0, keys, HD):
        key = norm_rotate_head(total[:, head : head + HD], cosine[part, :], sine[part, :])
        out[part, head : head + HD] = key.astype(out.dtype)
    out[part, keys:] = total[:, keys:].astype(out.dtype)


def finish_kernel(own_sum_a, own_a, far_a, far_b, early, cosine, sine, out):
    rows = own_a.shape[0]
    for index, far in enumerate((far_a, far_b)):
        at = index * rows
        total = early[at : at + rows, :].astype(jnp.float32) + far[...].astype(jnp.float32)
        finish(total, cosine, sine, out, at)
    finish(own_sum_a[...] + own_a[...].astype(jnp.float32), cosine, sine, out, 2 * rows)


def attend_kernel(group, q, done, own_sum_b, own_b, cosine, sine, allowed, out, kv):
    rows = q.shape[0]
    ready = done.shape[0]
    kv[:ready, :] = done[...]
    finish(own_sum_b[...] + own_b[...].astype(jnp.float32), cosine, sine, kv, ready)
    keys = kv.shape[1] // 2
    allow = jnp.concatenate([allowed[...]] * group, axis=0) > 0.5
    for head in range(0, keys, HD):
        key = kv[:, head : head + HD]
        value = kv[:, keys + head : keys + head + HD]
        at = head * group
        query = jnp.concatenate([q[:, at + g * HD : at + (g + 1) * HD] for g in range(group)], 0)
        scores = lax.dot_general(
            query, key, (((1,), (1,)), ((), ())), preferred_element_type=jnp.float32
        )
        weights = jnp.where(allow, jnp.exp(scores * (1.0 / HD**0.5)), 0.0)
        weights = weights.astype(jnp.bfloat16)
        total = jnp.sum(weights.astype(jnp.float32), axis=-1, keepdims=True)
        mixed = jnp.dot(weights, value, preferred_element_type=jnp.float32) / total
        mixed = mixed.astype(out.dtype)
        for g in range(group):
            out[:, at + g * HD : at + (g + 1) * HD] = mixed[g * rows : (g + 1) * rows, :]


def out_kernel(first, attended, w, stay, leave):
    half, wide = stay.shape
    block = 2 * HD
    for at in range(0, wide, block):
        part = pl.ds(first + at, block)
        total = jnp.dot(attended[...], w[:, part], preferred_element_type=jnp.float32)
        stay[:, at : at + block] = total[:half]
        leave[:, at : at + block] = total[half:].astype(leave.dtype)


def project_out(attended, w, first, wide):
    rows, depth = attended.shape
    return call(
        functools.partial(out_kernel, first),
        [shape(rows // 2, wide, jnp.float32), shape(rows // 2, wide, jnp.bfloat16)],
        16,
        2 * rows * depth * wide,
        2 * rows * depth,
    )(attended, w)


def on_four_by_two(inputs, doc_lengths, w_query, w_key, w_value, w_out):
    own = inputs[0]
    w_query, w_key, w_value, w_out = w_query[0], w_key[0], w_value[0], w_out[0]
    rows = own.shape[0]
    half = w_key.shape[0]
    group = w_query.shape[1] // w_key.shape[1]
    ctx, tp = lax.axis_index("ctx"), lax.axis_index("tp")
    block_rows = rows * lax.axis_size("tp")

    x_far = lax.dynamic_slice_in_dim(own, (1 - ctx) * half, half, 1)
    far_a = swap(x_far, "ctx", 1)
    x_near = lax.dynamic_slice_in_dim(after(own, x_far), ctx * half, half, 1)
    near_b = swap(x_near, "tp", 2)
    x_near_s = swap(x_near, "tp", 1)
    x_far_s = swap(x_far, "tp", 1)
    far_b = swap(far_a, "tp", 2)
    far_a_s = swap(far_a, "tp", 1)
    near_b_s = swap(near_b, "tp", 1)
    far_b_s = swap(far_b, "tp", 1)

    smem = pl.BlockSpec(memory_space=pltpu.SMEM)
    cosine, sine, allowed = call(
        functools.partial(tables_kernel, rows, block_rows),
        [
            shape(8 * rows, HD, jnp.float32),
            shape(8 * rows, HD, jnp.float32),
            shape(4 * rows, 8 * rows, jnp.float32),
        ],
        8,
        1 << 24,
        1 << 20,
        in_specs=[smem, smem],
    )(jnp.stack([ctx, tp]), doc_lengths)

    weights = [in_vmem(w_key), in_vmem(w_value)]
    own_sum_a, own_sum_b, own_send, far_sum_a = project_kv(
        [x_near, x_near_s, near_b, near_b_s, far_a, far_a_s],
        weights,
        [
            (0, 2 * rows, jnp.float32),
            (2 * rows, 4 * rows, jnp.float32),
            (0, 4 * rows, jnp.bfloat16),
            (4 * rows, 6 * rows, jnp.bfloat16),
        ],
    )
    early = lax.ppermute(own_send, "ctx", [(0, 1)])
    own_a = swap(far_sum_a, "ctx", 1)
    far_sum_b = project_kv([far_b, far_b_s], weights, [(0, 2 * rows, jnp.bfloat16)])[0]
    own_b = swap(far_sum_b, "ctx", 1)
    far_c = swap(x_far, "tp", 2)
    far_c_s = swap(far_c, "tp", 1)

    near = jnp.reshape(ctx, (1,))
    w_query = in_vmem(w_query)
    queries = project_query(near, [x_near, near_b, x_near_s, near_b_s], w_query)
    queries = project_query(
        1 - near, [x_far, far_c, x_far_s, far_c_s], w_query, queries, cosine, sine
    )

    kv_shape = shape(6 * rows, own_send.shape[1], jnp.bfloat16)
    done = call(finish_kernel, kv_shape, 8, 1 << 24, 1 << 20)(
        own_sum_a, own_a, far_sum_a, far_sum_b, early, cosine, sine
    )
    attended = call(
        functools.partial(attend_kernel, group),
        shape(4 * rows, queries.shape[1], jnp.bfloat16),
        16,
        8 * rows * 8 * rows * queries.shape[1],
        1 << 20,
        scratch_shapes=[pltpu.VMEM((8 * rows, own_send.shape[1]), jnp.bfloat16)],
    )(queries, done, own_sum_b, own_b, cosine, sine, allowed)

    w_out = in_vmem(w_out)
    wide = w_out.shape[1] // OUT_CHUNKS
    parts = []
    for chunk in range(OUT_CHUNKS):
        stay, leave = project_out(attended, w_out, chunk * wide, wide)
        stay = stay + swap(leave, "tp", 1).astype(jnp.float32)
        arrived = swap(stay[rows:].astype(jnp.bfloat16), "tp", 2)
        mixed = (stay[:rows] + arrived.astype(jnp.float32)).astype(jnp.bfloat16)
        parts.append(from_behind(mixed, "pipe", 1))
    return jnp.concatenate(parts, axis=1)[None]


def doc_index(positions, lengths):
    doc_ends = jnp.cumsum(lengths)
    return jnp.sum((positions[:, None] >= doc_ends[None, :]).astype(jnp.int32), axis=1)


def norm_rotate(entries, positions, head_count, head_width):
    row_count = entries.shape[0]
    shaped = entries.reshape(row_count, head_count, head_width)
    shaped = shaped * lax.rsqrt(jnp.mean(shaped * shaped, axis=-1, keepdims=True) + NORM_EPS)
    half_width = head_width // 2
    frequencies = jnp.power(
        ROPE_BASE, -(jnp.arange(half_width, dtype=jnp.float32) * 2.0 / head_width)
    )
    angles = positions.astype(jnp.float32)[:, None] * frequencies[None, :]
    cosine = jnp.cos(angles)[:, None, :]
    sine_part = jnp.sin(angles)[:, None, :]
    first_half = shaped[..., :half_width]
    second = shaped[..., half_width:]
    turned = jnp.concatenate(
        [first_half * cosine - second * sine_part, second * cosine + first_half * sine_part],
        axis=-1,
    )
    return turned.reshape(row_count, head_count * head_width)


def attend(queries, q_pos, q_doc, key_rows, value_rows, k_pos, k_doc):
    score_scale = 1.0 / HD**0.5
    scores = (
        jnp.einsum("tkgd,nkd->kgtn", queries, key_rows, preferred_element_type=jnp.float32)
        * score_scale
    )
    allowed = (
        (k_pos[None, :] <= q_pos[:, None])
        & (k_doc[None, :] == q_doc[:, None])
        & (k_pos[None, :] // SPAN == q_pos[:, None] // SPAN)
    )
    weights = jnp.where(allowed[None, None], jnp.exp(scores), 0.0).astype(jnp.bfloat16)
    numerator = jnp.einsum(
        "kgtn,nkd->tkgd", weights, value_rows, preferred_element_type=jnp.float32
    )
    denominator = jnp.sum(weights.astype(jnp.float32), axis=-1)
    return (numerator, denominator)


def on_any(inputs, doc_lengths, w_query, w_key, w_value, w_out):
    tok_rows = lax.all_gather(inputs[0], "tp", axis=0, tiled=True)
    block_rows = tok_rows.shape[0]
    q_heads = w_query.shape[2] // HD
    kv_heads = w_key.shape[2] // HD
    group_size = q_heads // kv_heads
    ctx_rank = lax.axis_index("ctx")
    positions = ctx_rank * block_rows + jnp.arange(block_rows, dtype=jnp.int32)
    lengths = doc_lengths[0]
    own_docs = doc_index(positions, lengths)
    queries = jnp.dot(tok_rows, w_query[0], preferred_element_type=jnp.float32)
    stacked_weights = jnp.stack([w_key[0], w_value[0]])
    key_value = jnp.einsum(
        "td,sdc->stc",
        tok_rows,
        lax.all_gather(stacked_weights, "ctx", axis=1, tiled=True),
        preferred_element_type=jnp.float32,
    )
    keys_float = key_value[0]
    values_float = key_value[1]
    q_round = (
        norm_rotate(queries, positions, q_heads, HD)
        .astype(jnp.bfloat16)
        .reshape(block_rows, kv_heads, group_size, HD)
    )
    k_round = norm_rotate(keys_float, positions, kv_heads, HD).astype(jnp.bfloat16)
    v_round = values_float.astype(jnp.bfloat16)
    key_value_pair = jnp.stack([k_round, v_round])
    shard_piece = lax.all_gather(key_value_pair, "ctx", axis=1, tiled=True)
    row_count = shard_piece.shape[1]
    k_pos = jnp.arange(row_count, dtype=jnp.int32)
    k_doc = doc_index(k_pos, lengths)
    key_rows = shard_piece[0].reshape(row_count, kv_heads, HD)
    value_rows = shard_piece[1].reshape(row_count, kv_heads, HD)
    numerator, denominator = attend(
        q_round, positions, own_docs, key_rows, value_rows, k_pos, k_doc
    )
    attended = (
        (numerator / jnp.transpose(denominator, (2, 0, 1))[..., None])
        .astype(jnp.bfloat16)
        .reshape(block_rows, q_heads * HD)
    )
    mixed = lax.psum_scatter(
        jnp.dot(attended, w_out[0], preferred_element_type=jnp.float32).astype(jnp.bfloat16),
        "tp",
        scatter_dimension=0,
        tiled=True,
    )
    return from_behind(mixed, "pipe", 1)[None]


def solution(mesh):
    in_specs = (
        P("pipe", ("ctx", "tp"), None),
        P("pipe", None),
        P("pipe", None, "tp"),
        P("pipe", "ctx", "tp"),
        P("pipe", "ctx", "tp"),
        P("pipe", "tp", None),
    )
    out_specs = P("pipe", ("ctx", "tp"), None)
    paired = mesh.shape["ctx"] == 2 and mesh.shape["tp"] == 4
    return jax.shard_map(
        on_four_by_two if paired else on_any,
        mesh=mesh,
        in_specs=in_specs,
        out_specs=out_specs,
        check_vma=False,
    )
```

```python
import functools
import math

import jax
import jax.numpy as jnp
from jax import lax
from jax.experimental import pallas as pl
from jax.experimental.pallas import tpu as pltpu
from jax.sharding import PartitionSpec as P

HD = 128
SPAN = 1024
ROPE_BASE = 500000.0
NORM_EPS = 1e-06
OUT_CHUNKS = 4
MIB = 1 << 20
VMEM_MIB = 16


def from_behind(value, axis, steps):
    count = lax.axis_size(axis)
    pairs = [(source, (source + steps) % count) for source in range(count)]
    return lax.ppermute(value, axis, pairs)


def swap(value, axis, bit):
    count = lax.axis_size(axis)
    return lax.ppermute(value, axis, [(source, source ^ bit) for source in range(count)])


def norm_rotate_head(head, cosine, sine):
    head = head * lax.rsqrt(jnp.mean(head * head, axis=-1, keepdims=True) + NORM_EPS)
    return head * cosine + pltpu.roll(head, HD // 2, 1) * sine


def shape(rows, columns, dtype):
    return jax.ShapeDtypeStruct((rows, columns), dtype)


def in_vmem(value):
    return pltpu.with_memory_space_constraint(value, pltpu.VMEM)


def in_hbm(value):
    return pltpu.with_memory_space_constraint(value, pltpu.HBM)


def call(kernel, out_shape, flops, moved, **given):
    return pl.pallas_call(
        kernel,
        out_shape=out_shape,
        compiler_params=pltpu.CompilerParams(vmem_limit_bytes=VMEM_MIB * MIB),
        cost_estimate=pl.CostEstimate(flops=flops, bytes_accessed=moved, transcendentals=0),
        **given,
    )


def after(value, *others):
    return lax.optimization_barrier((value, *others))[0]


def split_kernel(place, value, near, far, sems):
    wide = near.shape[1]
    at = pl.multiple_of(place[0] * wide, wide)
    near_copy = pltpu.make_async_copy(value.at[:, pl.ds(at, wide)], near, sems.at[0])
    far_copy = pltpu.make_async_copy(value.at[:, pl.ds(wide - at, wide)], far, sems.at[1])
    near_copy.start()
    far_copy.start()
    near_copy.wait()
    far_copy.wait()


def pass_kernel(count, *refs):
    for value, out in zip(refs[:count], refs[-count:]):
        out[...] = value[...]


def passed(values, *tokens):
    vmem, anywhere = pl.BlockSpec(memory_space=pltpu.VMEM), pl.BlockSpec(memory_space=pl.ANY)
    return call(
        functools.partial(pass_kernel, len(values)),
        [shape(*value.shape, value.dtype) for value in values],
        0,
        1 << 20,
        in_specs=[vmem] * len(values) + [anywhere] * len(tokens),
    )(*[in_vmem(value) for value in values], *tokens)


def fill_tables(rows, block_rows, place, lengths, cosine, sine, allowed):
    start, index = place[0] * block_rows, place[1]
    offsets = [start + shift + rows * (index ^ flip) for shift in (-block_rows, 0) for flip in range(4)]
    lane = lax.broadcasted_iota(jnp.int32, (1, HD), 1)
    power = (lane % (HD // 2)).astype(jnp.float32) * (2.0 / HD)
    frequency = jnp.exp(power * -math.log(ROPE_BASE))
    sign = jnp.where(lane < HD // 2, -1.0, 1.0)
    step = lax.broadcasted_iota(jnp.int32, (rows, HD), 0).astype(jnp.float32) * frequency
    step_cosine, step_sine = jnp.cos(step), jnp.sin(step)
    order = lax.broadcasted_iota(jnp.int32, (8, HD), 0)
    origin = jnp.zeros((8, HD), jnp.int32)
    for at, offset in enumerate(offsets):
        origin = jnp.where(order == at, offset, origin)
    origin = origin.astype(jnp.float32) * frequency
    origin_cosine, origin_sine = jnp.cos(origin), jnp.sin(origin)
    for at in range(8):
        part = pl.ds(at * rows, rows)
        far_cosine, far_sine = origin_cosine[at : at + 1, :], origin_sine[at : at + 1, :]
        cosine[part, :] = step_cosine * far_cosine - step_sine * far_sine
        sine[part, :] = (step_sine * far_cosine + step_cosine * far_sine) * sign

    row = lax.broadcasted_iota(jnp.int32, (rows, HD), 0)
    column = lax.broadcasted_iota(jnp.int32, (1, HD), 1)
    ends, end = [], 0
    for doc in range(lengths.shape[1]):
        end = end + lengths[0, doc]
        ends.append(end)
    for at in range(4):
        q_pos = row + offsets[4 + at]
        first = q_pos // SPAN * SPAN
        for end in ends:
            first = jnp.where(end <= q_pos, jnp.maximum(first, end), first)
        for to in range(0, 8 * rows, HD):
            k_pos = column + offsets[to // rows]
            for half in range(1, HD // rows):
                other = column + (offsets[to // rows + half] - half * rows)
                k_pos = jnp.where(column >= half * rows, other, k_pos)
            inside = (k_pos >= first) & (k_pos <= q_pos)
            allowed[at * rows : (at + 1) * rows, to : to + HD] = jnp.where(inside, 1.0, 0.0)


def stacked(pieces):
    return jnp.concatenate([piece[...] for piece in pieces], axis=0)


def put(total, to, *outs):
    for out in outs:
        out[:, to] = total.astype(out.dtype)


def own_kernel(block_rows, place, lengths, n0, n1, f0, f1, w_key, w_value, w, *refs):
    own_sum, own_send, query, key, value, w_near, w_far, cosine, sine, allowed, sems = refs
    piece, depth = n0.shape
    near_rows = w.at[pl.ds(pl.multiple_of(place[0] * depth, depth), depth)]
    far_rows = w.at[pl.ds(pl.multiple_of((1 - place[0]) * depth, depth), depth)]
    pairs = ((w_key, key), (w_value, value), (near_rows, w_near), (far_rows, w_far))
    copies = [pltpu.make_async_copy(*pair, sems.at[i]) for i, pair in enumerate(pairs)]
    for copy in copies:
        copy.start()
    fill_tables(piece, block_rows, place, lengths, cosine, sine, allowed)
    near, far = stacked((n0, n1)), stacked((f0, f1))
    wide = key.shape[1]
    for index, weight in enumerate((key, value)):
        copies[index].wait()
        total = jnp.dot(near, weight[...], preferred_element_type=jnp.float32)
        put(total, slice(index * wide, (index + 1) * wide), own_sum, own_send)
    block = 2 * HD
    copies[2].wait()
    columns = range(0, w.shape[1], block)
    first = [
        jnp.dot(near, w_near[:, at : at + block], preferred_element_type=jnp.float32)
        for at in columns
    ]
    copies[3].wait()
    turn = pl.ds(4 * piece, 2 * piece)
    for at, total in zip(columns, first):
        total += jnp.dot(far, w_far[:, at : at + block], preferred_element_type=jnp.float32)
        for head in range(0, block, HD):
            turned = norm_rotate_head(total[:, head : head + HD], cosine[turn, :], sine[turn, :])
            query[:, at + head : at + head + HD] = turned.astype(query.dtype)


def project_kernel(n0, n1, f0, f1, key, value, own_sum, own_send, far_sum):
    rows = stacked((n0, n1, f0, f1))
    whole, wide = own_sum.shape[0], key.shape[1]
    for index, weight in enumerate((key, value)):
        to = slice(index * wide, (index + 1) * wide)
        total = jnp.dot(rows, weight[...], preferred_element_type=jnp.float32)
        put(total[:whole], to, own_sum, own_send)
        put(total[whole:], to, far_sum)


def query_first_kernel(n0, n1, _, w, out):
    out[...] = jnp.dot(stacked((n0, n1)), w[...], preferred_element_type=jnp.float32)


def project_more_kernel(x0, x1, w0, w1, before, out):
    rows = stacked((x0, x1))
    ready, wide = before.shape[0], w0.shape[1]
    out[:ready, :] = before[...]
    for index, w in enumerate((w0, w1)):
        total = jnp.dot(rows, w[...], preferred_element_type=jnp.float32)
        out[ready:, index * wide : (index + 1) * wide] = total.astype(out.dtype)


def query_last_kernel(f0, f1, w, before, cosine, sine, out):
    rows = stacked((f0, f1))
    block = 2 * HD
    turn = pl.ds(3 * rows.shape[0], rows.shape[0])
    for at in range(0, w.shape[1], block):
        total = jnp.dot(rows, w[:, at : at + block], preferred_element_type=jnp.float32)
        total = total + before[:, at : at + block]
        for head in range(0, block, HD):
            query = norm_rotate_head(total[:, head : head + HD], cosine[turn, :], sine[turn, :])
            out[:, at + head : at + head + HD] = query.astype(out.dtype)


def finish(total, cosine, sine, out, at):
    rows, wide = total.shape
    keys = wide // 2
    part = pl.ds(at, rows)
    for head in range(0, keys, HD):
        key = norm_rotate_head(total[:, head : head + HD], cosine[part, :], sine[part, :])
        out[part, head : head + HD] = key.astype(out.dtype)
    out[part, keys:] = total[:, keys:].astype(out.dtype)


def finish_kernel(far, early_a, early_b, cosine, sine, out):
    rows = early_a.shape[0]
    for at, early in ((0, early_a), (rows, early_b)):
        total = early[...].astype(jnp.float32) + far[at : at + rows, :].astype(jnp.float32)
        finish(total, cosine, sine, out, at)


def attend_kernel(group, q_first, q_last, done, sum_a, sum_b, arrived, cosine, sine, allowed, out, kv):
    rows = 2 * q_first.shape[0]
    ready = done.shape[0]
    kv[:ready, :] = done[...]
    half = sum_a.shape[0]
    for at, own_sum in ((0, sum_a), (half, sum_b)):
        total = own_sum[...] + arrived[at : at + half, :].astype(jnp.float32)
        finish(total, cosine, sine, kv, ready + at)
    keys = kv.shape[1] // 2
    allow = jnp.concatenate([allowed[...]] * group, axis=0) > 0.5
    for head in range(0, keys, HD):
        key = kv[:, head : head + HD]
        value = kv[:, keys + head : keys + head + HD]
        at = head * group
        columns = [slice(at + g * HD, at + (g + 1) * HD) for g in range(group)]
        query = jnp.concatenate([q[:, c] for c in columns for q in (q_first, q_last)], 0)
        scores = lax.dot_general(
            query, key, (((1,), (1,)), ((), ())), preferred_element_type=jnp.float32
        )
        weights = jnp.where(allow, jnp.exp(scores * (1.0 / HD**0.5)), 0.0)
        weights = weights.astype(jnp.bfloat16)
        total = jnp.sum(weights.astype(jnp.float32), axis=-1, keepdims=True)
        mixed = jnp.dot(weights, value, preferred_element_type=jnp.float32) / total
        mixed = mixed.astype(out.dtype)
        for g, c in enumerate(columns):
            out[:, c] = mixed[g * rows : (g + 1) * rows, :]


def out_kernel(first, attended, w, stay, leave):
    wide = stay.shape[1]
    rows = stay.shape[0] // 2
    block = 2 * HD
    for at in range(0, wide, block):
        part = pl.ds(first + at, block)
        total = jnp.dot(attended[...], w[:, part], preferred_element_type=jnp.float32)
        for to, (index, out) in enumerate(((0, stay), (1, leave), (2, stay), (3, leave))):
            piece = total[index * rows : (index + 1) * rows].astype(out.dtype)
            out[to // 2 * rows : to // 2 * rows + rows, at : at + block] = piece


def project_out(attended, w, first, wide):
    rows, depth = attended.shape
    return call(
        functools.partial(out_kernel, first),
        [shape(rows // 2, wide, jnp.float32), shape(rows // 2, wide, jnp.bfloat16)],
        2 * rows * depth * wide,
        2 * rows * depth,
    )(attended, w)


def on_four_by_two(inputs, doc_lengths, w_query, w_key, w_value, w_out):
    own = inputs[0]
    w_query, w_key, w_value, w_out = w_query[0], w_key[0], w_value[0], w_out[0]
    rows = own.shape[0]
    half = w_key.shape[0]
    group = w_query.shape[1] // w_key.shape[1]
    ctx, tp = lax.axis_index("ctx"), lax.axis_index("tp")
    block_rows = rows * lax.axis_size("tp")

    smem, vmem = pl.BlockSpec(memory_space=pltpu.SMEM), pl.BlockSpec(memory_space=pltpu.VMEM)
    anywhere = pl.BlockSpec(memory_space=pl.ANY)

    place = jnp.stack([ctx, tp])
    x_near, x_far = call(
        split_kernel,
        [shape(rows, half, own.dtype)] * 2,
        0,
        1 << 20,
        in_specs=[smem, anywhere],
        scratch_shapes=[pltpu.SemaphoreType.DMA((2,))],
    )(place, in_hbm(own))
    far_a = swap(x_far, "ctx", 1)
    near_b = swap(x_near, "tp", 2)
    x_near_s = swap(x_near, "tp", 1)
    x_far_s = swap(x_far, "tp", 1)

    wide = w_query.shape[1]
    kv_wide = 2 * w_key.shape[1]
    kv_flops = 4 * rows * half * kv_wide
    sums = [shape(2 * rows, kv_wide, jnp.float32), shape(2 * rows, kv_wide, jnp.bfloat16)]
    sum_a, send_a, q_first, key, value, w_near, w_far, cosine, sine, allowed = call(
        functools.partial(own_kernel, block_rows),
        [
            *sums,
            shape(2 * rows, wide, jnp.bfloat16),
            *[shape(*w_key.shape, jnp.bfloat16)] * 2,
            *[shape(half, wide, jnp.bfloat16)] * 2,
            *[shape(8 * rows, HD, jnp.float32)] * 2,
            shape(4 * rows, 8 * rows, jnp.float32),
        ],
        kv_flops + 8 * rows * half * wide,
        8 * rows * half,
        in_specs=[smem] * 2 + [vmem] * 4 + [anywhere] * 3,
        scratch_shapes=[pltpu.SemaphoreType.DMA((4,))],
    )(
        place,
        doc_lengths,
        *(x_near, x_near_s, x_far, x_far_s),
        *(in_hbm(w_key), in_hbm(w_value), in_hbm(w_query)),
    )
    key, value, w_near, w_far = in_vmem(key), in_vmem(value), in_vmem(w_near), in_vmem(w_far)

    far_a, near_b, send_a = passed([far_a, near_b, send_a])
    far_b = swap(far_a, "tp", 2)
    early_a = swap(send_a, "ctx", 1)
    near_b_s = swap(near_b, "tp", 1)
    far_a_s = swap(far_a, "tp", 1)
    sum_b, send_b, far_sum_a = call(
        project_kernel, [*sums, sums[1]], 2 * kv_flops, 8 * rows * half
    )(near_b, near_b_s, far_a, far_a_s, key, value)
    early_b = swap(send_b, "ctx", 1)
    before = call(
        query_first_kernel,
        shape(2 * rows, wide, jnp.float32),
        4 * rows * half * wide,
        4 * rows * half,
        in_specs=[vmem] * 2 + [anywhere, vmem],
    )(near_b, near_b_s, send_b, w_near)

    x_again, far_b = passed([x_far, far_b], before, early_a, early_b)
    far_c = swap(x_again, "tp", 2)
    far_b_s = swap(far_b, "tp", 1)
    far_sum = call(
        project_more_kernel,
        shape(4 * rows, kv_wide, jnp.bfloat16),
        kv_flops,
        4 * rows * half,
    )(far_b, far_b_s, key, value, far_sum_a)
    arrived = swap(far_sum, "ctx", 1)
    far_c = passed([far_c], arrived)[0]
    far_c_s = swap(far_c, "tp", 1)
    q_last = call(
        query_last_kernel,
        shape(2 * rows, wide, jnp.bfloat16),
        4 * rows * half * wide,
        8 * rows * half,
    )(far_c, far_c_s, w_far, before, cosine, sine)

    kv_shape = shape(4 * rows, kv_wide, jnp.bfloat16)
    done = call(finish_kernel, kv_shape, 1 << 24, 1 << 20)(
        far_sum, early_a, early_b, cosine, sine
    )
    attended = call(
        functools.partial(attend_kernel, group),
        shape(4 * rows, wide, jnp.bfloat16),
        8 * rows * 8 * rows * wide,
        1 << 20,
        scratch_shapes=[pltpu.VMEM((8 * rows, kv_wide), jnp.bfloat16)],
    )(q_first, q_last, done, sum_a, sum_b, arrived, cosine, sine, allowed)

    w_out = in_vmem(w_out)
    wide = w_out.shape[1] // OUT_CHUNKS
    parts = []
    for chunk in range(OUT_CHUNKS):
        stay, leave = project_out(attended, w_out, chunk * wide, wide)
        stay = stay + swap(leave, "tp", 1).astype(jnp.float32)
        arrived = swap(stay[rows:].astype(jnp.bfloat16), "tp", 2)
        mixed = (stay[:rows] + arrived.astype(jnp.float32)).astype(jnp.bfloat16)
        parts.append(from_behind(mixed, "pipe", 1))
    return jnp.concatenate(parts, axis=1)[None]


def doc_index(positions, lengths):
    doc_ends = jnp.cumsum(lengths)
    return jnp.sum((positions[:, None] >= doc_ends[None, :]).astype(jnp.int32), axis=1)


def norm_rotate(entries, positions, head_count, head_width):
    row_count = entries.shape[0]
    shaped = entries.reshape(row_count, head_count, head_width)
    shaped = shaped * lax.rsqrt(jnp.mean(shaped * shaped, axis=-1, keepdims=True) + NORM_EPS)
    half_width = head_width // 2
    frequencies = jnp.power(
        ROPE_BASE, -(jnp.arange(half_width, dtype=jnp.float32) * 2.0 / head_width)
    )
    angles = positions.astype(jnp.float32)[:, None] * frequencies[None, :]
    cosine = jnp.cos(angles)[:, None, :]
    sine_part = jnp.sin(angles)[:, None, :]
    first_half = shaped[..., :half_width]
    second = shaped[..., half_width:]
    turned = jnp.concatenate(
        [first_half * cosine - second * sine_part, second * cosine + first_half * sine_part],
        axis=-1,
    )
    return turned.reshape(row_count, head_count * head_width)


def attend(queries, q_pos, q_doc, key_rows, value_rows, k_pos, k_doc):
    score_scale = 1.0 / HD**0.5
    scores = (
        jnp.einsum("tkgd,nkd->kgtn", queries, key_rows, preferred_element_type=jnp.float32)
        * score_scale
    )
    allowed = (
        (k_pos[None, :] <= q_pos[:, None])
        & (k_doc[None, :] == q_doc[:, None])
        & (k_pos[None, :] // SPAN == q_pos[:, None] // SPAN)
    )
    weights = jnp.where(allowed[None, None], jnp.exp(scores), 0.0).astype(jnp.bfloat16)
    numerator = jnp.einsum(
        "kgtn,nkd->tkgd", weights, value_rows, preferred_element_type=jnp.float32
    )
    denominator = jnp.sum(weights.astype(jnp.float32), axis=-1)
    return (numerator, denominator)


def on_any(inputs, doc_lengths, w_query, w_key, w_value, w_out):
    tok_rows = lax.all_gather(inputs[0], "tp", axis=0, tiled=True)
    block_rows = tok_rows.shape[0]
    q_heads = w_query.shape[2] // HD
    kv_heads = w_key.shape[2] // HD
    group_size = q_heads // kv_heads
    ctx_rank = lax.axis_index("ctx")
    positions = ctx_rank * block_rows + jnp.arange(block_rows, dtype=jnp.int32)
    lengths = doc_lengths[0]
    own_docs = doc_index(positions, lengths)
    queries = jnp.dot(tok_rows, w_query[0], preferred_element_type=jnp.float32)
    stacked_weights = jnp.stack([w_key[0], w_value[0]])
    key_value = jnp.einsum(
        "td,sdc->stc",
        tok_rows,
        lax.all_gather(stacked_weights, "ctx", axis=1, tiled=True),
        preferred_element_type=jnp.float32,
    )
    keys_float = key_value[0]
    values_float = key_value[1]
    q_round = (
        norm_rotate(queries, positions, q_heads, HD)
        .astype(jnp.bfloat16)
        .reshape(block_rows, kv_heads, group_size, HD)
    )
    k_round = norm_rotate(keys_float, positions, kv_heads, HD).astype(jnp.bfloat16)
    v_round = values_float.astype(jnp.bfloat16)
    key_value_pair = jnp.stack([k_round, v_round])
    shard_piece = lax.all_gather(key_value_pair, "ctx", axis=1, tiled=True)
    row_count = shard_piece.shape[1]
    k_pos = jnp.arange(row_count, dtype=jnp.int32)
    k_doc = doc_index(k_pos, lengths)
    key_rows = shard_piece[0].reshape(row_count, kv_heads, HD)
    value_rows = shard_piece[1].reshape(row_count, kv_heads, HD)
    numerator, denominator = attend(
        q_round, positions, own_docs, key_rows, value_rows, k_pos, k_doc
    )
    attended = (
        (numerator / jnp.transpose(denominator, (2, 0, 1))[..., None])
        .astype(jnp.bfloat16)
        .reshape(block_rows, q_heads * HD)
    )
    mixed = lax.psum_scatter(
        jnp.dot(attended, w_out[0], preferred_element_type=jnp.float32).astype(jnp.bfloat16),
        "tp",
        scatter_dimension=0,
        tiled=True,
    )
    return from_behind(mixed, "pipe", 1)[None]


def solution(mesh):
    in_specs = (
        P("pipe", ("ctx", "tp"), None),
        P("pipe", None),
        P("pipe", None, "tp"),
        P("pipe", "ctx", "tp"),
        P("pipe", "ctx", "tp"),
        P("pipe", "tp", None),
    )
    out_specs = P("pipe", ("ctx", "tp"), None)
    paired = mesh.shape["ctx"] == 2 and mesh.shape["tp"] == 4
    return jax.shard_map(
        on_four_by_two if paired else on_any,
        mesh=mesh,
        in_specs=in_specs,
        out_specs=out_specs,
        check_vma=False,
    )
```

```python
import functools
import math

import jax
import jax.numpy as jnp
from jax import lax
from jax.experimental import pallas as pl
from jax.experimental.pallas import tpu as pltpu
from jax.sharding import PartitionSpec as P

HD = 128
SPAN = 1024
ROPE_BASE = 500000.0
NORM_EPS = 1e-06
OUT_CHUNKS = 4
MIB = 1 << 20
VMEM_MIB = 16


def from_behind(value, axis, steps):
    count = lax.axis_size(axis)
    pairs = [(source, (source + steps) % count) for source in range(count)]
    return lax.ppermute(value, axis, pairs)


def swap(value, axis, bit):
    count = lax.axis_size(axis)
    return lax.ppermute(value, axis, [(source, source ^ bit) for source in range(count)])


def norm_rotate_head(head, cosine, sine):
    head = head * lax.rsqrt(jnp.mean(head * head, axis=-1, keepdims=True) + NORM_EPS)
    return head * cosine + pltpu.roll(head, HD // 2, 1) * sine


def shape(rows, columns, dtype):
    return jax.ShapeDtypeStruct((rows, columns), dtype)


def in_vmem(value):
    return pltpu.with_memory_space_constraint(value, pltpu.VMEM)


def in_hbm(value):
    return pltpu.with_memory_space_constraint(value, pltpu.HBM)


def call(kernel, out_shape, flops, moved, **given):
    return pl.pallas_call(
        kernel,
        out_shape=out_shape,
        compiler_params=pltpu.CompilerParams(vmem_limit_bytes=VMEM_MIB * MIB),
        cost_estimate=pl.CostEstimate(flops=flops, bytes_accessed=moved, transcendentals=0),
        **given,
    )


def after(value, *others):
    return lax.optimization_barrier((value, *others))[0]


def split_kernel(place, value, near, far, sems):
    wide = near.shape[1]
    at = pl.multiple_of(place[0] * wide, wide)
    near_copy = pltpu.make_async_copy(value.at[:, pl.ds(at, wide)], near, sems.at[0])
    far_copy = pltpu.make_async_copy(value.at[:, pl.ds(wide - at, wide)], far, sems.at[1])
    near_copy.start()
    far_copy.start()
    near_copy.wait()
    far_copy.wait()


def pass_kernel(ranges, *refs):
    count = len(ranges)
    for value, out, (start, stop) in zip(refs[:count], refs[-count:], ranges):
        out[...] = value[:, start:stop]


def passed(values, *tokens, ranges=None):
    vmem, anywhere = pl.BlockSpec(memory_space=pltpu.VMEM), pl.BlockSpec(memory_space=pl.ANY)
    ranges = ranges or [(0, value.shape[1]) for value in values]
    return call(
        functools.partial(pass_kernel, ranges),
        [
            shape(value.shape[0], stop - start, value.dtype)
            for value, (start, stop) in zip(values, ranges)
        ],
        0,
        1 << 20,
        in_specs=[vmem] * len(values) + [anywhere] * len(tokens),
    )(*[in_vmem(value) for value in values], *tokens)


def split_columns(wide, count):
    tiles = wide // HD
    cuts = [tiles * at // count * HD for at in range(count + 1)]
    return list(zip(cuts[:-1], cuts[1:]))


def fill_tables(rows, block_rows, place, lengths, cosine, sine, allowed):
    start, index = place[0] * block_rows, place[1]
    offsets = [start + shift + rows * (index ^ flip) for shift in (-block_rows, 0) for flip in range(4)]
    lane = lax.broadcasted_iota(jnp.int32, (1, HD), 1)
    power = (lane % (HD // 2)).astype(jnp.float32) * (2.0 / HD)
    frequency = jnp.exp(power * -math.log(ROPE_BASE))
    sign = jnp.where(lane < HD // 2, -1.0, 1.0)
    step = lax.broadcasted_iota(jnp.int32, (rows, HD), 0).astype(jnp.float32) * frequency
    step_cosine, step_sine = jnp.cos(step), jnp.sin(step)
    order = lax.broadcasted_iota(jnp.int32, (8, HD), 0)
    origin = jnp.zeros((8, HD), jnp.int32)
    for at, offset in enumerate(offsets):
        origin = jnp.where(order == at, offset, origin)
    origin = origin.astype(jnp.float32) * frequency
    origin_cosine, origin_sine = jnp.cos(origin), jnp.sin(origin)
    for at in range(8):
        part = pl.ds(at * rows, rows)
        far_cosine, far_sine = origin_cosine[at : at + 1, :], origin_sine[at : at + 1, :]
        cosine[part, :] = step_cosine * far_cosine - step_sine * far_sine
        sine[part, :] = (step_sine * far_cosine + step_cosine * far_sine) * sign

    row = lax.broadcasted_iota(jnp.int32, (rows, HD), 0)
    column = lax.broadcasted_iota(jnp.int32, (1, HD), 1)
    ends, end = [], 0
    for doc in range(lengths.shape[1]):
        end = end + lengths[0, doc]
        ends.append(end)
    for at in range(4):
        q_pos = row + offsets[4 + at]
        first = q_pos // SPAN * SPAN
        for end in ends:
            first = jnp.where(end <= q_pos, jnp.maximum(first, end), first)
        for to in range(0, 8 * rows, HD):
            k_pos = column + offsets[to // rows]
            for half in range(1, HD // rows):
                other = column + (offsets[to // rows + half] - half * rows)
                k_pos = jnp.where(column >= half * rows, other, k_pos)
            inside = (k_pos >= first) & (k_pos <= q_pos)
            allowed[at * rows : (at + 1) * rows, to : to + HD] = jnp.where(inside, 1.0, 0.0)


def stacked(pieces):
    return jnp.concatenate([piece[...] for piece in pieces], axis=0)


def stacked_parts(own, parts):
    other = jnp.concatenate([part[...] for part in parts], axis=1) if len(parts) > 1 else parts[0][...]
    return jnp.concatenate([own[...], other], axis=0)


def put(total, to, *outs):
    for out in outs:
        out[:, to] = total.astype(out.dtype)


def own_kernel(block_rows, place, lengths, n0, n1, f0, f1, w_key, w_value, w, *refs):
    own_sum, own_send, query, key, value, w_near, w_far, cosine, sine, allowed, sems = refs
    piece, depth = n0.shape
    near_rows = w.at[pl.ds(pl.multiple_of(place[0] * depth, depth), depth)]
    far_rows = w.at[pl.ds(pl.multiple_of((1 - place[0]) * depth, depth), depth)]
    pairs = ((w_key, key), (w_value, value), (near_rows, w_near), (far_rows, w_far))
    copies = [pltpu.make_async_copy(*pair, sems.at[i]) for i, pair in enumerate(pairs)]
    for copy in copies:
        copy.start()
    fill_tables(piece, block_rows, place, lengths, cosine, sine, allowed)
    near, far = stacked((n0, n1)), stacked((f0, f1))
    wide = key.shape[1]
    for index, weight in enumerate((key, value)):
        copies[index].wait()
        total = jnp.dot(near, weight[...], preferred_element_type=jnp.float32)
        put(total, slice(index * wide, (index + 1) * wide), own_sum, own_send)
    block = 2 * HD
    copies[2].wait()
    columns = range(0, w.shape[1], block)
    first = [
        jnp.dot(near, w_near[:, at : at + block], preferred_element_type=jnp.float32)
        for at in columns
    ]
    copies[3].wait()
    turn = pl.ds(4 * piece, 2 * piece)
    for at, total in zip(columns, first):
        total += jnp.dot(far, w_far[:, at : at + block], preferred_element_type=jnp.float32)
        for head in range(0, block, HD):
            turned = norm_rotate_head(total[:, head : head + HD], cosine[turn, :], sine[turn, :])
            query[:, at + head : at + head + HD] = turned.astype(query.dtype)


def project_kernel(n0, n1, f0, f1, key, value, own_sum, send, rest):
    rows = stacked((n0, n1, f0, f1))
    whole, ready, wide = own_sum.shape[0], send.shape[0], key.shape[1]
    for index, weight in enumerate((key, value)):
        to = slice(index * wide, (index + 1) * wide)
        total = jnp.dot(rows, weight[...], preferred_element_type=jnp.float32)
        put(total[:whole], to, own_sum)
        put(total[:ready], to, send)
        put(total[ready:], to, rest)


def query_first_kernel(n0, n1, _, w, out):
    out[...] = jnp.dot(stacked((n0, n1)), w[...], preferred_element_type=jnp.float32)


def project_more_kernel(before, x0, w0, w1, *refs):
    rows, out = stacked_parts(x0, refs[:-1]), refs[-1]
    ready, wide = before.shape[0], w0.shape[1]
    out[:ready, :] = before[...]
    for index, w in enumerate((w0, w1)):
        total = jnp.dot(rows, w[...], preferred_element_type=jnp.float32)
        out[ready:, index * wide : (index + 1) * wide] = total.astype(out.dtype)


def query_last_kernel(f0, w, before, cosine, sine, *refs):
    rows, out = stacked_parts(f0, refs[:-1]), refs[-1]
    block = 2 * HD
    turn = pl.ds(3 * rows.shape[0], rows.shape[0])
    for at in range(0, w.shape[1], block):
        total = jnp.dot(rows, w[:, at : at + block], preferred_element_type=jnp.float32)
        total = total + before[:, at : at + block]
        for head in range(0, block, HD):
            query = norm_rotate_head(total[:, head : head + HD], cosine[turn, :], sine[turn, :])
            out[:, at + head : at + head + HD] = query.astype(out.dtype)


def finish(total, cosine, sine, out, at):
    rows, wide = total.shape
    keys = wide // 2
    part = pl.ds(at, rows)
    for head in range(0, keys, HD):
        key = norm_rotate_head(total[:, head : head + HD], cosine[part, :], sine[part, :])
        out[part, head : head + HD] = key.astype(out.dtype)
    out[part, keys:] = total[:, keys:].astype(out.dtype)


def finish_kernel(send, far, early_a, early_b, cosine, sine, out):
    rows = early_a.shape[0]
    early = jnp.concatenate([early_a[...], early_b[:rows, :]], axis=0)
    far = jnp.concatenate([send[rows:, :], far[...]], axis=0)
    finish(early.astype(jnp.float32) + far.astype(jnp.float32), cosine, sine, out, 0)


def attend_kernel(group, q_first, q_last, done, sum_a, sum_b, more_a, more_b, cosine, sine, allowed, out, kv):
    rows = 2 * q_first.shape[0]
    ready = done.shape[0]
    kv[:ready, :] = done[...]
    half = sum_a.shape[0]
    total = jnp.concatenate([sum_a[...], sum_b[...]], axis=0)
    more = jnp.concatenate([more_a[half:, :], more_b[...]], axis=0)
    finish(total + more.astype(jnp.float32), cosine, sine, kv, ready)
    keys = kv.shape[1] // 2
    allow = jnp.concatenate([allowed[...]] * group, axis=0) > 0.5
    for head in range(0, keys, HD):
        key = kv[:, head : head + HD]
        value = kv[:, keys + head : keys + head + HD]
        at = head * group
        columns = [slice(at + g * HD, at + (g + 1) * HD) for g in range(group)]
        query = jnp.concatenate([q[:, c] for c in columns for q in (q_first, q_last)], 0)
        scores = lax.dot_general(
            query, key, (((1,), (1,)), ((), ())), preferred_element_type=jnp.float32
        )
        weights = jnp.where(allow, jnp.exp(scores * (1.0 / HD**0.5)), 0.0)
        weights = weights.astype(jnp.bfloat16)
        total = jnp.sum(weights.astype(jnp.float32), axis=-1, keepdims=True)
        mixed = jnp.dot(weights, value, preferred_element_type=jnp.float32) / total
        mixed = mixed.astype(out.dtype)
        for g, c in enumerate(columns):
            out[:, c] = mixed[g * rows : (g + 1) * rows, :]


def out_kernel(first, attended, w, stay, leave):
    wide = stay.shape[1]
    rows = stay.shape[0] // 2
    block = 2 * HD
    for at in range(0, wide, block):
        part = pl.ds(first + at, block)
        total = jnp.dot(attended[...], w[:, part], preferred_element_type=jnp.float32)
        for to, (index, out) in enumerate(((0, stay), (1, leave), (2, stay), (3, leave))):
            piece = total[index * rows : (index + 1) * rows].astype(out.dtype)
            out[to // 2 * rows : to // 2 * rows + rows, at : at + block] = piece


def project_out(attended, w, first, wide):
    rows, depth = attended.shape
    return call(
        functools.partial(out_kernel, first),
        [shape(rows // 2, wide, jnp.float32), shape(rows // 2, wide, jnp.bfloat16)],
        2 * rows * depth * wide,
        2 * rows * depth,
    )(attended, w)


def on_four_by_two(inputs, doc_lengths, w_query, w_key, w_value, w_out):
    own = inputs[0]
    w_query, w_key, w_value, w_out = w_query[0], w_key[0], w_value[0], w_out[0]
    rows = own.shape[0]
    half = w_key.shape[0]
    group = w_query.shape[1] // w_key.shape[1]
    ctx, tp = lax.axis_index("ctx"), lax.axis_index("tp")
    block_rows = rows * lax.axis_size("tp")

    smem, vmem = pl.BlockSpec(memory_space=pltpu.SMEM), pl.BlockSpec(memory_space=pltpu.VMEM)
    anywhere = pl.BlockSpec(memory_space=pl.ANY)

    place = jnp.stack([ctx, tp])
    x_near, x_far = call(
        split_kernel,
        [shape(rows, half, own.dtype)] * 2,
        0,
        1 << 20,
        in_specs=[smem, anywhere],
        scratch_shapes=[pltpu.SemaphoreType.DMA((2,))],
    )(place, in_hbm(own))
    far_a = swap(x_far, "ctx", 1)
    near_b = swap(x_near, "tp", 2)
    x_near_s = swap(x_near, "tp", 1)
    x_far_s = swap(x_far, "tp", 1)

    wide = w_query.shape[1]
    kv_wide = 2 * w_key.shape[1]
    kv_flops = 4 * rows * half * kv_wide
    sums = [shape(2 * rows, kv_wide, jnp.float32), shape(2 * rows, kv_wide, jnp.bfloat16)]
    sum_a, send_a, q_first, key, value, w_near, w_far, cosine, sine, allowed = call(
        functools.partial(own_kernel, block_rows),
        [
            *sums,
            shape(2 * rows, wide, jnp.bfloat16),
            *[shape(*w_key.shape, jnp.bfloat16)] * 2,
            *[shape(half, wide, jnp.bfloat16)] * 2,
            *[shape(8 * rows, HD, jnp.float32)] * 2,
            shape(4 * rows, 8 * rows, jnp.float32),
        ],
        kv_flops + 8 * rows * half * wide,
        8 * rows * half,
        in_specs=[smem] * 2 + [vmem] * 4 + [anywhere] * 3,
        scratch_shapes=[pltpu.SemaphoreType.DMA((4,))],
    )(
        place,
        doc_lengths,
        *(x_near, x_near_s, x_far, x_far_s),
        *(in_hbm(w_key), in_hbm(w_value), in_hbm(w_query)),
    )
    key, value, w_near, w_far = in_vmem(key), in_vmem(value), in_vmem(w_near), in_vmem(w_far)

    far_a, near_b, send_a = passed([far_a, near_b, send_a])
    far_b = swap(far_a, "tp", 2)
    early_a = swap(send_a, "ctx", 1)
    near_b_s = swap(near_b, "tp", 1)
    far_a_s = swap(far_a, "tp", 1)
    sum_b, send_b, rest = call(
        project_kernel,
        [sums[0], shape(3 * rows, kv_wide, jnp.bfloat16), shape(rows, kv_wide, jnp.bfloat16)],
        2 * kv_flops,
        8 * rows * half,
    )(near_b, near_b_s, far_a, far_a_s, key, value)
    early_b = swap(send_b, "ctx", 1)
    before = call(
        query_first_kernel,
        shape(2 * rows, wide, jnp.float32),
        4 * rows * half * wide,
        4 * rows * half,
        in_specs=[vmem] * 2 + [anywhere, vmem],
    )(near_b, near_b_s, early_a, w_near)

    far_c = swap(passed([x_far], before)[0], "tp", 2)
    parts = split_columns(half, 2)
    far_b, *pieces = passed(
        [far_b] * (len(parts) + 1), before, early_b, ranges=[(0, half), *parts]
    )
    pieces = [swap(piece, "tp", 1) for piece in pieces]
    far_sum_b = call(
        project_more_kernel,
        shape(3 * rows, kv_wide, jnp.bfloat16),
        kv_flops,
        4 * rows * half,
    )(rest, far_b, key, value, *pieces)
    more_b = swap(far_sum_b, "ctx", 1)
    parts = split_columns(half, 3)
    pieces = passed([far_c] * len(parts), far_sum_b, ranges=parts)
    pieces = [swap(piece, "tp", 1) for piece in pieces]
    q_last = call(
        query_last_kernel,
        shape(2 * rows, wide, jnp.bfloat16),
        4 * rows * half * wide,
        8 * rows * half,
    )(far_c, w_far, before, cosine, sine, *pieces)

    kv_shape = shape(4 * rows, kv_wide, jnp.bfloat16)
    done = call(finish_kernel, kv_shape, 1 << 24, 1 << 20)(
        send_b, far_sum_b, early_a, early_b, cosine, sine
    )
    attended = call(
        functools.partial(attend_kernel, group),
        shape(4 * rows, wide, jnp.bfloat16),
        8 * rows * 8 * rows * wide,
        1 << 20,
        scratch_shapes=[pltpu.VMEM((8 * rows, kv_wide), jnp.bfloat16)],
    )(q_first, q_last, done, sum_a, sum_b, early_b, more_b, cosine, sine, allowed)

    w_out = in_vmem(w_out)
    wide = w_out.shape[1] // OUT_CHUNKS
    parts = []
    for chunk in range(OUT_CHUNKS):
        stay, leave = project_out(attended, w_out, chunk * wide, wide)
        stay = stay + swap(leave, "tp", 1).astype(jnp.float32)
        arrived = swap(stay[rows:].astype(jnp.bfloat16), "tp", 2)
        mixed = (stay[:rows] + arrived.astype(jnp.float32)).astype(jnp.bfloat16)
        parts.append(from_behind(mixed, "pipe", 1))
    return jnp.concatenate(parts, axis=1)[None]


def doc_index(positions, lengths):
    doc_ends = jnp.cumsum(lengths)
    return jnp.sum((positions[:, None] >= doc_ends[None, :]).astype(jnp.int32), axis=1)


def norm_rotate(entries, positions, head_count, head_width):
    row_count = entries.shape[0]
    shaped = entries.reshape(row_count, head_count, head_width)
    shaped = shaped * lax.rsqrt(jnp.mean(shaped * shaped, axis=-1, keepdims=True) + NORM_EPS)
    half_width = head_width // 2
    frequencies = jnp.power(
        ROPE_BASE, -(jnp.arange(half_width, dtype=jnp.float32) * 2.0 / head_width)
    )
    angles = positions.astype(jnp.float32)[:, None] * frequencies[None, :]
    cosine = jnp.cos(angles)[:, None, :]
    sine_part = jnp.sin(angles)[:, None, :]
    first_half = shaped[..., :half_width]
    second = shaped[..., half_width:]
    turned = jnp.concatenate(
        [first_half * cosine - second * sine_part, second * cosine + first_half * sine_part],
        axis=-1,
    )
    return turned.reshape(row_count, head_count * head_width)


def attend(queries, q_pos, q_doc, key_rows, value_rows, k_pos, k_doc):
    score_scale = 1.0 / HD**0.5
    scores = (
        jnp.einsum("tkgd,nkd->kgtn", queries, key_rows, preferred_element_type=jnp.float32)
        * score_scale
    )
    allowed = (
        (k_pos[None, :] <= q_pos[:, None])
        & (k_doc[None, :] == q_doc[:, None])
        & (k_pos[None, :] // SPAN == q_pos[:, None] // SPAN)
    )
    weights = jnp.where(allowed[None, None], jnp.exp(scores), 0.0).astype(jnp.bfloat16)
    numerator = jnp.einsum(
        "kgtn,nkd->tkgd", weights, value_rows, preferred_element_type=jnp.float32
    )
    denominator = jnp.sum(weights.astype(jnp.float32), axis=-1)
    return (numerator, denominator)


def on_any(inputs, doc_lengths, w_query, w_key, w_value, w_out):
    tok_rows = lax.all_gather(inputs[0], "tp", axis=0, tiled=True)
    block_rows = tok_rows.shape[0]
    q_heads = w_query.shape[2] // HD
    kv_heads = w_key.shape[2] // HD
    group_size = q_heads // kv_heads
    ctx_rank = lax.axis_index("ctx")
    positions = ctx_rank * block_rows + jnp.arange(block_rows, dtype=jnp.int32)
    lengths = doc_lengths[0]
    own_docs = doc_index(positions, lengths)
    queries = jnp.dot(tok_rows, w_query[0], preferred_element_type=jnp.float32)
    stacked_weights = jnp.stack([w_key[0], w_value[0]])
    key_value = jnp.einsum(
        "td,sdc->stc",
        tok_rows,
        lax.all_gather(stacked_weights, "ctx", axis=1, tiled=True),
        preferred_element_type=jnp.float32,
    )
    keys_float = key_value[0]
    values_float = key_value[1]
    q_round = (
        norm_rotate(queries, positions, q_heads, HD)
        .astype(jnp.bfloat16)
        .reshape(block_rows, kv_heads, group_size, HD)
    )
    k_round = norm_rotate(keys_float, positions, kv_heads, HD).astype(jnp.bfloat16)
    v_round = values_float.astype(jnp.bfloat16)
    key_value_pair = jnp.stack([k_round, v_round])
    shard_piece = lax.all_gather(key_value_pair, "ctx", axis=1, tiled=True)
    row_count = shard_piece.shape[1]
    k_pos = jnp.arange(row_count, dtype=jnp.int32)
    k_doc = doc_index(k_pos, lengths)
    key_rows = shard_piece[0].reshape(row_count, kv_heads, HD)
    value_rows = shard_piece[1].reshape(row_count, kv_heads, HD)
    numerator, denominator = attend(
        q_round, positions, own_docs, key_rows, value_rows, k_pos, k_doc
    )
    attended = (
        (numerator / jnp.transpose(denominator, (2, 0, 1))[..., None])
        .astype(jnp.bfloat16)
        .reshape(block_rows, q_heads * HD)
    )
    mixed = lax.psum_scatter(
        jnp.dot(attended, w_out[0], preferred_element_type=jnp.float32).astype(jnp.bfloat16),
        "tp",
        scatter_dimension=0,
        tiled=True,
    )
    return from_behind(mixed, "pipe", 1)[None]


def solution(mesh):
    in_specs = (
        P("pipe", ("ctx", "tp"), None),
        P("pipe", None),
        P("pipe", None, "tp"),
        P("pipe", "ctx", "tp"),
        P("pipe", "ctx", "tp"),
        P("pipe", "tp", None),
    )
    out_specs = P("pipe", ("ctx", "tp"), None)
    paired = mesh.shape["ctx"] == 2 and mesh.shape["tp"] == 4
    return jax.shard_map(
        on_four_by_two if paired else on_any,
        mesh=mesh,
        in_specs=in_specs,
        out_specs=out_specs,
        check_vma=False,
    )
```

```python
import functools
import math

import jax
import jax.numpy as jnp
from jax import lax
from jax.experimental import pallas as pl
from jax.experimental.pallas import tpu as pltpu
from jax.sharding import PartitionSpec as P

HD = 128
SPAN = 1024
ROPE_BASE = 500000.0
NORM_EPS = 1e-06
OUT_CHUNKS = 5
MIB = 1 << 20
VMEM_MIB = 16


def from_behind(value, axis, steps):
    count = lax.axis_size(axis)
    pairs = [(source, (source + steps) % count) for source in range(count)]
    return lax.ppermute(value, axis, pairs)


def swap(value, axis, bit):
    count = lax.axis_size(axis)
    return lax.ppermute(value, axis, [(source, source ^ bit) for source in range(count)])


def norm_rotate_head(head, cosine, sine):
    head = head * lax.rsqrt(jnp.mean(head * head, axis=-1, keepdims=True) + NORM_EPS)
    return head * cosine + pltpu.roll(head, HD // 2, 1) * sine


def shape(rows, columns, dtype):
    return jax.ShapeDtypeStruct((rows, columns), dtype)


def in_vmem(value):
    return pltpu.with_memory_space_constraint(value, pltpu.VMEM)


def in_hbm(value):
    return pltpu.with_memory_space_constraint(value, pltpu.HBM)


def call(kernel, out_shape, flops, moved, **given):
    return pl.pallas_call(
        kernel,
        out_shape=out_shape,
        compiler_params=pltpu.CompilerParams(vmem_limit_bytes=VMEM_MIB * MIB),
        cost_estimate=pl.CostEstimate(flops=flops, bytes_accessed=moved, transcendentals=0),
        **given,
    )


def split_kernel(value, near, far, sems):
    wide = near.shape[1]
    at = pl.multiple_of(lax.axis_index("ctx") * wide, wide)
    near_copy = pltpu.make_async_copy(value.at[:, pl.ds(at, wide)], near, sems.at[0])
    far_copy = pltpu.make_async_copy(value.at[:, pl.ds(wide - at, wide)], far, sems.at[1])
    near_copy.start()
    far_copy.start()
    near_copy.wait()
    far_copy.wait()


def pass_kernel(ranges, *refs):
    count = len(ranges)
    for value, out, (start, stop) in zip(refs[:count], refs[-count:], ranges):
        out[...] = value[:, start:stop]


def passed(values, *tokens, ranges=None):
    vmem, anywhere = pl.BlockSpec(memory_space=pltpu.VMEM), pl.BlockSpec(memory_space=pl.ANY)
    ranges = ranges or [(0, value.shape[1]) for value in values]
    return call(
        functools.partial(pass_kernel, ranges),
        [
            shape(value.shape[0], stop - start, value.dtype)
            for value, (start, stop) in zip(values, ranges)
        ],
        0,
        1 << 20,
        in_specs=[vmem] * len(values) + [anywhere] * len(tokens),
    )(*[in_vmem(value) for value in values], *tokens)


def split_columns(wide, count):
    tiles = wide // HD
    cuts = [tiles * at // count * HD for at in range(count + 1)]
    return list(zip(cuts[:-1], cuts[1:]))


def fill_tables(rows, block_rows, lengths, cosine, sine, allowed):
    start, index = lax.axis_index("ctx") * block_rows, lax.axis_index("tp")
    offsets = [start + shift + rows * (index ^ flip) for shift in (-block_rows, 0) for flip in range(4)]
    lane = lax.broadcasted_iota(jnp.int32, (1, HD), 1)
    power = (lane % (HD // 2)).astype(jnp.float32) * (2.0 / HD)
    frequency = jnp.exp(power * -math.log(ROPE_BASE))
    sign = jnp.where(lane < HD // 2, -1.0, 1.0)
    step = lax.broadcasted_iota(jnp.int32, (rows, HD), 0).astype(jnp.float32) * frequency
    step_cosine, step_sine = jnp.cos(step), jnp.sin(step)
    order = lax.broadcasted_iota(jnp.int32, (8, HD), 0)
    origin = jnp.zeros((8, HD), jnp.int32)
    for at, offset in enumerate(offsets):
        origin = jnp.where(order == at, offset, origin)
    origin = origin.astype(jnp.float32) * frequency
    origin_cosine, origin_sine = jnp.cos(origin), jnp.sin(origin)
    for at in range(8):
        part = pl.ds(at * rows, rows)
        far_cosine, far_sine = origin_cosine[at : at + 1, :], origin_sine[at : at + 1, :]
        cosine[part, :] = step_cosine * far_cosine - step_sine * far_sine
        sine[part, :] = (step_sine * far_cosine + step_cosine * far_sine) * sign

    row = lax.broadcasted_iota(jnp.int32, (rows, HD), 0)
    column = lax.broadcasted_iota(jnp.int32, (1, HD), 1)
    ends, end = [], 0
    for doc in range(lengths.shape[1]):
        end = end + lengths[0, doc]
        ends.append(end)
    for at in range(4):
        q_pos = row + offsets[4 + at]
        first = q_pos // SPAN * SPAN
        for end in ends:
            first = jnp.where(end <= q_pos, jnp.maximum(first, end), first)
        for to in range(0, 8 * rows, HD):
            k_pos = column + offsets[to // rows]
            for half in range(1, HD // rows):
                other = column + (offsets[to // rows + half] - half * rows)
                k_pos = jnp.where(column >= half * rows, other, k_pos)
            inside = (k_pos >= first) & (k_pos <= q_pos)
            allowed[at * rows : (at + 1) * rows, to : to + HD] = jnp.where(inside, 1.0, 0.0)


def stacked(pieces):
    return jnp.concatenate([piece[...] for piece in pieces], axis=0)


def stacked_parts(own, parts):
    other = jnp.concatenate([part[...] for part in parts], axis=1) if len(parts) > 1 else parts[0][...]
    return jnp.concatenate([own[...], other], axis=0)


def put(total, to, *outs):
    for out in outs:
        out[:, to] = total.astype(out.dtype)


def own_kernel(block_rows, lengths, n0, n1, f0, f1, w_key, w_value, w, *refs):
    own_sum, own_send, query, key, value, w_near, w_far, cosine, sine, allowed, sems = refs
    piece, depth = n0.shape
    ctx = lax.axis_index("ctx")
    near_rows = w.at[pl.ds(pl.multiple_of(ctx * depth, depth), depth)]
    far_rows = w.at[pl.ds(pl.multiple_of((1 - ctx) * depth, depth), depth)]
    pairs = ((w_key, key), (w_value, value), (near_rows, w_near), (far_rows, w_far))
    copies = [pltpu.make_async_copy(*pair, sems.at[i]) for i, pair in enumerate(pairs)]
    for copy in copies:
        copy.start()
    fill_tables(piece, block_rows, lengths, cosine, sine, allowed)
    near, far = stacked((n0, n1)), stacked((f0, f1))
    wide = key.shape[1]
    for index, weight in enumerate((key, value)):
        copies[index].wait()
        total = jnp.dot(near, weight[...], preferred_element_type=jnp.float32)
        put(total, slice(index * wide, (index + 1) * wide), own_sum, own_send)
    block = 2 * HD
    copies[2].wait()
    columns = range(0, w.shape[1], block)
    first = [
        jnp.dot(near, w_near[:, at : at + block], preferred_element_type=jnp.float32)
        for at in columns
    ]
    copies[3].wait()
    turn = pl.ds(4 * piece, 2 * piece)
    for at, total in zip(columns, first):
        total += jnp.dot(far, w_far[:, at : at + block], preferred_element_type=jnp.float32)
        for head in range(0, block, HD):
            turned = norm_rotate_head(total[:, head : head + HD], cosine[turn, :], sine[turn, :])
            query[:, at + head : at + head + HD] = turned.astype(query.dtype)


def project_kernel(n0, n1, f0, f1, key, value, own_sum, send, rest):
    rows = stacked((n0, n1, f0, f1))
    whole, ready, wide = own_sum.shape[0], send.shape[0], key.shape[1]
    for index, weight in enumerate((key, value)):
        to = slice(index * wide, (index + 1) * wide)
        total = jnp.dot(rows, weight[...], preferred_element_type=jnp.float32)
        put(total[:whole], to, own_sum)
        put(total[:ready], to, send)
        put(total[ready:], to, rest)


def query_first_kernel(n0, n1, _, w, out):
    out[...] = jnp.dot(stacked((n0, n1)), w[...], preferred_element_type=jnp.float32)


def project_more_kernel(before, x0, w0, w1, *refs):
    rows, out = stacked_parts(x0, refs[:-1]), refs[-1]
    ready, wide = before.shape[0], w0.shape[1]
    out[:ready, :] = before[...]
    for index, w in enumerate((w0, w1)):
        total = jnp.dot(rows, w[...], preferred_element_type=jnp.float32)
        out[ready:, index * wide : (index + 1) * wide] = total.astype(out.dtype)


def query_last_kernel(f0, w, before, cosine, sine, *refs):
    rows, out = stacked_parts(f0, refs[:-1]), refs[-1]
    block = 2 * HD
    turn = pl.ds(3 * rows.shape[0], rows.shape[0])
    for at in range(0, w.shape[1], block):
        total = jnp.dot(rows, w[:, at : at + block], preferred_element_type=jnp.float32)
        total = total + before[:, at : at + block]
        for head in range(0, block, HD):
            query = norm_rotate_head(total[:, head : head + HD], cosine[turn, :], sine[turn, :])
            out[:, at + head : at + head + HD] = query.astype(out.dtype)


def finish(total, cosine, sine, out, at):
    rows, wide = total.shape
    keys = wide // 2
    part = pl.ds(at, rows)
    for head in range(0, keys, HD):
        key = norm_rotate_head(total[:, head : head + HD], cosine[part, :], sine[part, :])
        out[part, head : head + HD] = key.astype(out.dtype)
    out[part, keys:] = total[:, keys:].astype(out.dtype)


def finish_kernel(send, far, early_a, early_b, cosine, sine, out):
    rows = early_a.shape[0]
    early = jnp.concatenate([early_a[...], early_b[:rows, :]], axis=0)
    far = jnp.concatenate([send[rows:, :], far[...]], axis=0)
    finish(early.astype(jnp.float32) + far.astype(jnp.float32), cosine, sine, out, 0)


def attend_kernel(group, q_first, q_last, done, sum_a, sum_b, more_a, more_b, cosine, sine, allowed, out, kv):
    rows = 2 * q_first.shape[0]
    ready = done.shape[0]
    kv[:ready, :] = done[...]
    half = sum_a.shape[0]
    total = jnp.concatenate([sum_a[...], sum_b[...]], axis=0)
    more = jnp.concatenate([more_a[half:, :], more_b[...]], axis=0)
    finish(total + more.astype(jnp.float32), cosine, sine, kv, ready)
    keys = kv.shape[1] // 2
    allow = jnp.concatenate([allowed[...]] * group, axis=0) > 0.5
    for head in range(0, keys, HD):
        key = kv[:, head : head + HD]
        value = kv[:, keys + head : keys + head + HD]
        at = head * group
        columns = [slice(at + g * HD, at + (g + 1) * HD) for g in range(group)]
        query = jnp.concatenate([q[:, c] for c in columns for q in (q_first, q_last)], 0)
        scores = lax.dot_general(
            query, key, (((1,), (1,)), ((), ())), preferred_element_type=jnp.float32
        )
        weights = jnp.where(allow, jnp.exp(scores * (1.0 / HD**0.5)), 0.0)
        weights = weights.astype(jnp.bfloat16)
        total = jnp.sum(weights.astype(jnp.float32), axis=-1, keepdims=True)
        mixed = jnp.dot(weights, value, preferred_element_type=jnp.float32) / total
        mixed = mixed.astype(out.dtype)
        for g, c in enumerate(columns):
            out[:, c] = mixed[g * rows : (g + 1) * rows, :]


def out_kernel(attended, w, *refs):
    stays, leaves = refs[::2], refs[1::2]
    half, wide = stays[0].shape
    rows = half // 2
    block = 2 * HD
    for chunk, (stay, leave) in enumerate(zip(stays, leaves)):
        for at in range(0, wide, block):
            part = pl.ds(chunk * wide + at, block)
            total = jnp.dot(attended[...], w[:, part], preferred_element_type=jnp.float32)
            for to, (index, out) in enumerate(((0, stay), (1, leave), (2, stay), (3, leave))):
                piece = total[index * rows : (index + 1) * rows].astype(out.dtype)
                out[to // 2 * rows : to // 2 * rows + rows, at : at + block] = piece


def project_out(attended, w, chunks):
    rows, depth = attended.shape
    wide = w.shape[1] // chunks
    pair = [shape(rows // 2, wide, jnp.float32), shape(rows // 2, wide, jnp.bfloat16)]
    outs = call(out_kernel, pair * chunks, 2 * rows * depth * w.shape[1], 2 * rows * depth)(
        attended, w
    )
    return list(zip(outs[::2], outs[1::2]))


def mix_kernel(stay, arrived, out):
    out[...] = (stay[...] + arrived[...].astype(jnp.float32)).astype(out.dtype)


def mix(stay, arrived):
    return call(mix_kernel, shape(*arrived.shape, arrived.dtype), 0, 1 << 20)(stay, arrived)


def on_four_by_two(inputs, doc_lengths, w_query, w_key, w_value, w_out):
    own = inputs[0]
    w_query, w_key, w_value, w_out = w_query[0], w_key[0], w_value[0], w_out[0]
    rows = own.shape[0]
    half = w_key.shape[0]
    group = w_query.shape[1] // w_key.shape[1]
    block_rows = rows * lax.axis_size("tp")

    smem, vmem = pl.BlockSpec(memory_space=pltpu.SMEM), pl.BlockSpec(memory_space=pltpu.VMEM)
    anywhere = pl.BlockSpec(memory_space=pl.ANY)

    x_near, x_far = call(
        split_kernel,
        [shape(rows, half, own.dtype)] * 2,
        0,
        1 << 20,
        in_specs=[anywhere],
        scratch_shapes=[pltpu.SemaphoreType.DMA((2,))],
    )(in_hbm(own))
    far_a = swap(x_far, "ctx", 1)
    near_b = swap(x_near, "tp", 2)
    x_near_s = swap(x_near, "tp", 1)
    x_far_s = swap(x_far, "tp", 1)

    wide = w_query.shape[1]
    kv_wide = 2 * w_key.shape[1]
    kv_flops = 4 * rows * half * kv_wide
    sums = [shape(2 * rows, kv_wide, jnp.float32), shape(2 * rows, kv_wide, jnp.bfloat16)]
    sum_a, send_a, q_first, key, value, w_near, w_far, cosine, sine, allowed = call(
        functools.partial(own_kernel, block_rows),
        [
            *sums,
            shape(2 * rows, wide, jnp.bfloat16),
            *[shape(*w_key.shape, jnp.bfloat16)] * 2,
            *[shape(half, wide, jnp.bfloat16)] * 2,
            *[shape(8 * rows, HD, jnp.float32)] * 2,
            shape(4 * rows, 8 * rows, jnp.float32),
        ],
        kv_flops + 8 * rows * half * wide,
        8 * rows * half,
        in_specs=[smem] + [vmem] * 4 + [anywhere] * 3,
        scratch_shapes=[pltpu.SemaphoreType.DMA((4,))],
    )(
        in_hbm(doc_lengths),
        *(x_near, x_near_s, x_far, x_far_s),
        *(in_hbm(w_key), in_hbm(w_value), in_hbm(w_query)),
    )
    key, value, w_near, w_far = in_vmem(key), in_vmem(value), in_vmem(w_near), in_vmem(w_far)

    far_a, near_b, send_a = passed([far_a, near_b, send_a])
    far_b = swap(far_a, "tp", 2)
    early_a = swap(send_a, "ctx", 1)
    near_b_s = swap(near_b, "tp", 1)
    far_a_s = swap(far_a, "tp", 1)
    sum_b, send_b, rest = call(
        project_kernel,
        [sums[0], shape(3 * rows, kv_wide, jnp.bfloat16), shape(rows, kv_wide, jnp.bfloat16)],
        2 * kv_flops,
        8 * rows * half,
    )(near_b, near_b_s, far_a, far_a_s, key, value)
    early_b = swap(send_b, "ctx", 1)
    before = call(
        query_first_kernel,
        shape(2 * rows, wide, jnp.float32),
        4 * rows * half * wide,
        4 * rows * half,
        in_specs=[vmem] * 2 + [anywhere, vmem],
    )(near_b, near_b_s, early_a, w_near)

    far_c = swap(passed([x_far], before)[0], "tp", 2)
    parts = split_columns(half, 2)
    far_b, *pieces = passed(
        [far_b] * (len(parts) + 1), before, early_b, ranges=[(0, half), *parts]
    )
    pieces = [swap(piece, "tp", 1) for piece in pieces]
    far_sum_b = call(
        project_more_kernel,
        shape(3 * rows, kv_wide, jnp.bfloat16),
        kv_flops,
        4 * rows * half,
    )(rest, far_b, key, value, *pieces)
    more_b = swap(far_sum_b, "ctx", 1)
    parts = split_columns(half, 3)
    pieces = passed([far_c] * len(parts), far_sum_b, ranges=parts)
    pieces = [swap(piece, "tp", 1) for piece in pieces]
    q_last = call(
        query_last_kernel,
        shape(2 * rows, wide, jnp.bfloat16),
        4 * rows * half * wide,
        8 * rows * half,
    )(far_c, w_far, before, cosine, sine, *pieces)

    kv_shape = shape(4 * rows, kv_wide, jnp.bfloat16)
    done = call(finish_kernel, kv_shape, 1 << 24, 1 << 20)(
        send_b, far_sum_b, early_a, early_b, cosine, sine
    )
    attended = call(
        functools.partial(attend_kernel, group),
        shape(4 * rows, wide, jnp.bfloat16),
        8 * rows * 8 * rows * wide,
        1 << 20,
        scratch_shapes=[pltpu.VMEM((8 * rows, kv_wide), jnp.bfloat16)],
    )(q_first, q_last, done, sum_a, sum_b, early_b, more_b, cosine, sine, allowed)

    w_out = in_vmem(w_out)
    out, first = jnp.zeros((rows, w_out.shape[1]), jnp.bfloat16), 0
    for stay, leave in project_out(attended, w_out, OUT_CHUNKS):
        stay = stay + swap(leave, "tp", 1).astype(jnp.float32)
        arrived = swap(stay[rows:].astype(jnp.bfloat16), "tp", 2)
        part = from_behind(mix(stay[:rows], arrived), "pipe", 1)
        out = lax.dynamic_update_slice(out, part, (0, first))
        first += part.shape[1]
    return out[None]


def doc_index(positions, lengths):
    doc_ends = jnp.cumsum(lengths)
    return jnp.sum((positions[:, None] >= doc_ends[None, :]).astype(jnp.int32), axis=1)


def norm_rotate(entries, positions, head_count, head_width):
    row_count = entries.shape[0]
    shaped = entries.reshape(row_count, head_count, head_width)
    shaped = shaped * lax.rsqrt(jnp.mean(shaped * shaped, axis=-1, keepdims=True) + NORM_EPS)
    half_width = head_width // 2
    frequencies = jnp.power(
        ROPE_BASE, -(jnp.arange(half_width, dtype=jnp.float32) * 2.0 / head_width)
    )
    angles = positions.astype(jnp.float32)[:, None] * frequencies[None, :]
    cosine = jnp.cos(angles)[:, None, :]
    sine_part = jnp.sin(angles)[:, None, :]
    first_half = shaped[..., :half_width]
    second = shaped[..., half_width:]
    turned = jnp.concatenate(
        [first_half * cosine - second * sine_part, second * cosine + first_half * sine_part],
        axis=-1,
    )
    return turned.reshape(row_count, head_count * head_width)


def attend(queries, q_pos, q_doc, key_rows, value_rows, k_pos, k_doc):
    score_scale = 1.0 / HD**0.5
    scores = (
        jnp.einsum("tkgd,nkd->kgtn", queries, key_rows, preferred_element_type=jnp.float32)
        * score_scale
    )
    allowed = (
        (k_pos[None, :] <= q_pos[:, None])
        & (k_doc[None, :] == q_doc[:, None])
        & (k_pos[None, :] // SPAN == q_pos[:, None] // SPAN)
    )
    weights = jnp.where(allowed[None, None], jnp.exp(scores), 0.0).astype(jnp.bfloat16)
    numerator = jnp.einsum(
        "kgtn,nkd->tkgd", weights, value_rows, preferred_element_type=jnp.float32
    )
    denominator = jnp.sum(weights.astype(jnp.float32), axis=-1)
    return (numerator, denominator)


def on_any(inputs, doc_lengths, w_query, w_key, w_value, w_out):
    tok_rows = lax.all_gather(inputs[0], "tp", axis=0, tiled=True)
    block_rows = tok_rows.shape[0]
    q_heads = w_query.shape[2] // HD
    kv_heads = w_key.shape[2] // HD
    group_size = q_heads // kv_heads
    ctx_rank = lax.axis_index("ctx")
    positions = ctx_rank * block_rows + jnp.arange(block_rows, dtype=jnp.int32)
    lengths = doc_lengths[0]
    own_docs = doc_index(positions, lengths)
    queries = jnp.dot(tok_rows, w_query[0], preferred_element_type=jnp.float32)
    stacked_weights = jnp.stack([w_key[0], w_value[0]])
    key_value = jnp.einsum(
        "td,sdc->stc",
        tok_rows,
        lax.all_gather(stacked_weights, "ctx", axis=1, tiled=True),
        preferred_element_type=jnp.float32,
    )
    keys_float = key_value[0]
    values_float = key_value[1]
    q_round = (
        norm_rotate(queries, positions, q_heads, HD)
        .astype(jnp.bfloat16)
        .reshape(block_rows, kv_heads, group_size, HD)
    )
    k_round = norm_rotate(keys_float, positions, kv_heads, HD).astype(jnp.bfloat16)
    v_round = values_float.astype(jnp.bfloat16)
    key_value_pair = jnp.stack([k_round, v_round])
    shard_piece = lax.all_gather(key_value_pair, "ctx", axis=1, tiled=True)
    row_count = shard_piece.shape[1]
    k_pos = jnp.arange(row_count, dtype=jnp.int32)
    k_doc = doc_index(k_pos, lengths)
    key_rows = shard_piece[0].reshape(row_count, kv_heads, HD)
    value_rows = shard_piece[1].reshape(row_count, kv_heads, HD)
    numerator, denominator = attend(
        q_round, positions, own_docs, key_rows, value_rows, k_pos, k_doc
    )
    attended = (
        (numerator / jnp.transpose(denominator, (2, 0, 1))[..., None])
        .astype(jnp.bfloat16)
        .reshape(block_rows, q_heads * HD)
    )
    mixed = lax.psum_scatter(
        jnp.dot(attended, w_out[0], preferred_element_type=jnp.float32).astype(jnp.bfloat16),
        "tp",
        scatter_dimension=0,
        tiled=True,
    )
    return from_behind(mixed, "pipe", 1)[None]


def solution(mesh):
    in_specs = (
        P("pipe", ("ctx", "tp"), None),
        P("pipe", None),
        P("pipe", None, "tp"),
        P("pipe", "ctx", "tp"),
        P("pipe", "ctx", "tp"),
        P("pipe", "tp", None),
    )
    out_specs = P("pipe", ("ctx", "tp"), None)
    paired = mesh.shape["ctx"] == 2 and mesh.shape["tp"] == 4
    return jax.shard_map(
        on_four_by_two if paired else on_any,
        mesh=mesh,
        in_specs=in_specs,
        out_specs=out_specs,
        check_vma=False,
    )
```

```python
import functools
import math

import jax
import jax.numpy as jnp
from jax import lax
from jax.experimental import pallas as pl
from jax.experimental.pallas import tpu as pltpu
from jax.sharding import PartitionSpec as P

HD = 128
SPAN = 1024
ROPE_BASE = 500000.0
NORM_EPS = 1e-06
MASKED = -1e30
OUT_CHUNKS = 5
MIB = 1 << 20
VMEM_MIB = 16


def from_behind(value, axis, steps):
    count = lax.axis_size(axis)
    pairs = [(source, (source + steps) % count) for source in range(count)]
    return lax.ppermute(value, axis, pairs)


def swap(value, axis, bit):
    count = lax.axis_size(axis)
    return lax.ppermute(value, axis, [(source, source ^ bit) for source in range(count)])


def norm_rotate_head(head, cosine, sine):
    head = head * lax.rsqrt(jnp.mean(head * head, axis=-1, keepdims=True) + NORM_EPS)
    return head * cosine + pltpu.roll(head, HD // 2, 1) * sine


def shape(rows, columns, dtype):
    return jax.ShapeDtypeStruct((rows, columns), dtype)


def in_vmem(value):
    return pltpu.with_memory_space_constraint(value, pltpu.VMEM)


def in_hbm(value):
    return pltpu.with_memory_space_constraint(value, pltpu.HBM)


def call(kernel, out_shape, flops, moved, **given):
    return pl.pallas_call(
        kernel,
        out_shape=out_shape,
        compiler_params=pltpu.CompilerParams(vmem_limit_bytes=VMEM_MIB * MIB),
        cost_estimate=pl.CostEstimate(flops=flops, bytes_accessed=moved, transcendentals=0),
        **given,
    )


def split_kernel(value, near, far, sems):
    wide = near.shape[1]
    at = pl.multiple_of(lax.axis_index("ctx") * wide, wide)
    near_copy = pltpu.make_async_copy(value.at[:, pl.ds(at, wide)], near, sems.at[0])
    far_copy = pltpu.make_async_copy(value.at[:, pl.ds(wide - at, wide)], far, sems.at[1])
    near_copy.start()
    far_copy.start()
    near_copy.wait()
    far_copy.wait()


def pass_kernel(ranges, *refs):
    count = len(ranges)
    for value, out, (start, stop) in zip(refs[:count], refs[-count:], ranges):
        out[...] = value[:, start:stop]


def passed(values, *tokens, ranges=None):
    vmem, anywhere = pl.BlockSpec(memory_space=pltpu.VMEM), pl.BlockSpec(memory_space=pl.ANY)
    ranges = ranges or [(0, value.shape[1]) for value in values]
    return call(
        functools.partial(pass_kernel, ranges),
        [
            shape(value.shape[0], stop - start, value.dtype)
            for value, (start, stop) in zip(values, ranges)
        ],
        0,
        1 << 20,
        in_specs=[vmem] * len(values) + [anywhere] * len(tokens),
    )(*[in_vmem(value) for value in values], *tokens)


def split_columns(wide, count):
    tiles = wide // HD
    cuts = [tiles * at // count * HD for at in range(count + 1)]
    return list(zip(cuts[:-1], cuts[1:]))


def fill_tables(rows, block_rows, lengths, cosine, sine, allowed):
    start, index = lax.axis_index("ctx") * block_rows, lax.axis_index("tp")
    offsets = [start + shift + rows * (index ^ flip) for shift in (-block_rows, 0) for flip in range(4)]
    lane = lax.broadcasted_iota(jnp.int32, (1, HD), 1)
    power = (lane % (HD // 2)).astype(jnp.float32) * (2.0 / HD)
    frequency = jnp.exp(power * -math.log(ROPE_BASE))
    sign = jnp.where(lane < HD // 2, -1.0, 1.0)
    step = lax.broadcasted_iota(jnp.int32, (rows, HD), 0).astype(jnp.float32) * frequency
    step_cosine, step_sine = jnp.cos(step), jnp.sin(step)
    order = lax.broadcasted_iota(jnp.int32, (8, HD), 0)
    origin = jnp.zeros((8, HD), jnp.int32)
    for at, offset in enumerate(offsets):
        origin = jnp.where(order == at, offset, origin)
    origin = origin.astype(jnp.float32) * frequency
    origin_cosine, origin_sine = jnp.cos(origin), jnp.sin(origin)
    for at in range(8):
        part = pl.ds(at * rows, rows)
        far_cosine, far_sine = origin_cosine[at : at + 1, :], origin_sine[at : at + 1, :]
        cosine[part, :] = step_cosine * far_cosine - step_sine * far_sine
        sine[part, :] = (step_sine * far_cosine + step_cosine * far_sine) * sign

    row = lax.broadcasted_iota(jnp.int32, (rows, HD), 0)
    column = lax.broadcasted_iota(jnp.int32, (1, HD), 1)
    ends, end = [], 0
    for doc in range(lengths.shape[1]):
        end = end + lengths[0, doc]
        ends.append(end)
    for at in range(4):
        q_pos = row + offsets[4 + at]
        first = q_pos // SPAN * SPAN
        for end in ends:
            first = jnp.where(end <= q_pos, jnp.maximum(first, end), first)
        for to in range(0, 8 * rows, HD):
            k_pos = column + offsets[to // rows]
            for half in range(1, HD // rows):
                other = column + (offsets[to // rows + half] - half * rows)
                k_pos = jnp.where(column >= half * rows, other, k_pos)
            inside = (k_pos >= first) & (k_pos <= q_pos)
            allowed[at * rows : (at + 1) * rows, to : to + HD] = jnp.where(inside, 0.0, MASKED)


def stacked(pieces):
    return jnp.concatenate([piece[...] for piece in pieces], axis=0)


def stacked_parts(own, parts):
    other = jnp.concatenate([part[...] for part in parts], axis=1) if len(parts) > 1 else parts[0][...]
    return jnp.concatenate([own[...], other], axis=0)


def put(total, to, *outs):
    for out in outs:
        out[:, to] = total.astype(out.dtype)


def own_kernel(block_rows, lengths, n0, n1, f0, f1, w_key, w_value, w, *refs):
    own_sum, own_send, query, key, value, w_near, w_far, cosine, sine, allowed, sems = refs
    piece, depth = n0.shape
    ctx = lax.axis_index("ctx")
    near_rows = w.at[pl.ds(pl.multiple_of(ctx * depth, depth), depth)]
    far_rows = w.at[pl.ds(pl.multiple_of((1 - ctx) * depth, depth), depth)]
    pairs = ((w_key, key), (w_value, value), (near_rows, w_near), (far_rows, w_far))
    copies = [pltpu.make_async_copy(*pair, sems.at[i]) for i, pair in enumerate(pairs)]
    for copy in copies:
        copy.start()
    fill_tables(piece, block_rows, lengths, cosine, sine, allowed)
    near, far = stacked((n0, n1)), stacked((f0, f1))
    wide = key.shape[1]
    for index, weight in enumerate((key, value)):
        copies[index].wait()
        total = jnp.dot(near, weight[...], preferred_element_type=jnp.float32)
        put(total, slice(index * wide, (index + 1) * wide), own_sum, own_send)
    block = 2 * HD
    copies[2].wait()
    columns = range(0, w.shape[1], block)
    first = [
        jnp.dot(near, w_near[:, at : at + block], preferred_element_type=jnp.float32)
        for at in columns
    ]
    copies[3].wait()
    turn = pl.ds(4 * piece, 2 * piece)
    for at, total in zip(columns, first):
        total += jnp.dot(far, w_far[:, at : at + block], preferred_element_type=jnp.float32)
        for head in range(0, block, HD):
            turned = norm_rotate_head(total[:, head : head + HD], cosine[turn, :], sine[turn, :])
            query[:, at + head : at + head + HD] = turned.astype(query.dtype)


def project_kernel(n0, n1, f0, f1, key, value, own_sum, send, rest):
    rows = stacked((n0, n1, f0, f1))
    whole, ready, wide = own_sum.shape[0], send.shape[0], key.shape[1]
    for index, weight in enumerate((key, value)):
        to = slice(index * wide, (index + 1) * wide)
        total = jnp.dot(rows, weight[...], preferred_element_type=jnp.float32)
        put(total[:whole], to, own_sum)
        put(total[:ready], to, send)
        put(total[ready:], to, rest)


def query_first_kernel(n0, n1, _, w, out):
    out[...] = jnp.dot(stacked((n0, n1)), w[...], preferred_element_type=jnp.float32)


def project_more_kernel(before, x0, w0, w1, *refs):
    rows, out = stacked_parts(x0, refs[:-1]), refs[-1]
    ready, wide = before.shape[0], w0.shape[1]
    out[:ready, :] = before[...]
    for index, w in enumerate((w0, w1)):
        total = jnp.dot(rows, w[...], preferred_element_type=jnp.float32)
        out[ready:, index * wide : (index + 1) * wide] = total.astype(out.dtype)


def query_last_kernel(f0, w, before, cosine, sine, *refs):
    rows, out = stacked_parts(f0, refs[:-1]), refs[-1]
    block = 2 * HD
    turn = pl.ds(3 * rows.shape[0], rows.shape[0])
    for at in range(0, w.shape[1], block):
        total = jnp.dot(rows, w[:, at : at + block], preferred_element_type=jnp.float32)
        total = total + before[:, at : at + block]
        for head in range(0, block, HD):
            query = norm_rotate_head(total[:, head : head + HD], cosine[turn, :], sine[turn, :])
            out[:, at + head : at + head + HD] = query.astype(out.dtype)


def finish(total, cosine, sine, out, at):
    rows, wide = total.shape
    keys = wide // 2
    part = pl.ds(at, rows)
    for head in range(0, keys, HD):
        key = norm_rotate_head(total[:, head : head + HD], cosine[part, :], sine[part, :])
        out[part, head : head + HD] = key.astype(out.dtype)
    out[part, keys:] = total[:, keys:].astype(out.dtype)


def finish_kernel(send, far, early_a, early_b, cosine, sine, out):
    rows = early_a.shape[0]
    early = jnp.concatenate([early_a[...], early_b[:rows, :]], axis=0)
    far = jnp.concatenate([send[rows:, :], far[...]], axis=0)
    finish(early.astype(jnp.float32) + far.astype(jnp.float32), cosine, sine, out, 0)


def attend_kernel(group, q_first, q_last, done, sum_a, sum_b, more_a, more_b, cosine, sine, allowed, out, kv):
    rows = 2 * q_first.shape[0]
    ready = done.shape[0]
    kv[:ready, :] = done[...]
    half = sum_a.shape[0]
    total = jnp.concatenate([sum_a[...], sum_b[...]], axis=0)
    more = jnp.concatenate([more_a[half:, :], more_b[...]], axis=0)
    finish(total + more.astype(jnp.float32), cosine, sine, kv, ready)
    keys = kv.shape[1] // 2
    bias = jnp.concatenate([allowed[...]] * group, axis=0)
    ones = jnp.ones((kv.shape[0], HD), kv.dtype)
    for head in range(0, keys, HD):
        key = kv[:, head : head + HD]
        value = kv[:, keys + head : keys + head + HD]
        at = head * group
        columns = [slice(at + g * HD, at + (g + 1) * HD) for g in range(group)]
        query = jnp.concatenate([q[:, c] for c in columns for q in (q_first, q_last)], 0)
        scores = lax.dot_general(
            query, key, (((1,), (1,)), ((), ())), preferred_element_type=jnp.float32
        )
        weights = jnp.exp(scores * (1.0 / HD**0.5) + bias).astype(jnp.bfloat16)
        value = jnp.concatenate([value, ones], axis=1)
        mixed = jnp.dot(weights, value, preferred_element_type=jnp.float32)
        mixed = (mixed[:, :HD] / mixed[:, HD:]).astype(out.dtype)
        for g, c in enumerate(columns):
            out[:, c] = mixed[g * rows : (g + 1) * rows, :]


def out_kernel(first, attended, w, *refs):
    stays, leaves = refs[::2], refs[1::2]
    half, wide = stays[0].shape
    rows = half // 2
    block = 2 * HD
    for chunk, (stay, leave) in enumerate(zip(stays, leaves)):
        for at in range(0, wide, block):
            part = pl.ds((first + chunk) * wide + at, block)
            total = jnp.dot(attended[...], w[:, part], preferred_element_type=jnp.float32)
            for to, (index, out) in enumerate(((0, stay), (1, leave), (2, stay), (3, leave))):
                piece = total[index * rows : (index + 1) * rows].astype(out.dtype)
                out[to // 2 * rows : to // 2 * rows + rows, at : at + block] = piece


def project_out(attended, w, first, chunks):
    rows, depth = attended.shape
    wide = w.shape[1] // OUT_CHUNKS
    pair = [shape(rows // 2, wide, jnp.float32), shape(rows // 2, wide, jnp.bfloat16)]
    outs = call(
        functools.partial(out_kernel, first),
        pair * chunks,
        2 * rows * depth * wide * chunks,
        2 * rows * depth,
    )(attended, w)
    return list(zip(outs[::2], outs[1::2]))


def mix_kernel(stay, arrived, out):
    out[...] = (stay[...] + arrived[...].astype(jnp.float32)).astype(out.dtype)


def mix(stay, arrived):
    return call(mix_kernel, shape(*arrived.shape, arrived.dtype), 0, 1 << 20)(stay, arrived)


def on_four_by_two(inputs, doc_lengths, w_query, w_key, w_value, w_out):
    own = inputs[0]
    w_query, w_key, w_value, w_out = w_query[0], w_key[0], w_value[0], w_out[0]
    rows = own.shape[0]
    half = w_key.shape[0]
    group = w_query.shape[1] // w_key.shape[1]
    block_rows = rows * lax.axis_size("tp")

    smem, vmem = pl.BlockSpec(memory_space=pltpu.SMEM), pl.BlockSpec(memory_space=pltpu.VMEM)
    anywhere = pl.BlockSpec(memory_space=pl.ANY)

    x_near, x_far = call(
        split_kernel,
        [shape(rows, half, own.dtype)] * 2,
        0,
        1 << 20,
        in_specs=[anywhere],
        scratch_shapes=[pltpu.SemaphoreType.DMA((2,))],
    )(in_hbm(own))
    far_a = swap(x_far, "ctx", 1)
    near_b = swap(x_near, "tp", 2)
    x_near_s = swap(x_near, "tp", 1)
    x_far_s = swap(x_far, "tp", 1)

    wide = w_query.shape[1]
    kv_wide = 2 * w_key.shape[1]
    kv_flops = 4 * rows * half * kv_wide
    sums = [shape(2 * rows, kv_wide, jnp.float32), shape(2 * rows, kv_wide, jnp.bfloat16)]
    sum_a, send_a, q_first, key, value, w_near, w_far, cosine, sine, allowed = call(
        functools.partial(own_kernel, block_rows),
        [
            *sums,
            shape(2 * rows, wide, jnp.bfloat16),
            *[shape(*w_key.shape, jnp.bfloat16)] * 2,
            *[shape(half, wide, jnp.bfloat16)] * 2,
            *[shape(8 * rows, HD, jnp.float32)] * 2,
            shape(4 * rows, 8 * rows, jnp.float32),
        ],
        kv_flops + 8 * rows * half * wide,
        8 * rows * half,
        in_specs=[smem] + [vmem] * 4 + [anywhere] * 3,
        scratch_shapes=[pltpu.SemaphoreType.DMA((4,))],
    )(
        in_hbm(doc_lengths),
        *(x_near, x_near_s, x_far, x_far_s),
        *(in_hbm(w_key), in_hbm(w_value), in_hbm(w_query)),
    )
    key, value, w_near, w_far = in_vmem(key), in_vmem(value), in_vmem(w_near), in_vmem(w_far)

    far_a, near_b, send_a = passed([far_a, near_b, send_a])
    far_b = swap(far_a, "tp", 2)
    early_a = swap(send_a, "ctx", 1)
    near_b_s = swap(near_b, "tp", 1)
    far_a_s = swap(far_a, "tp", 1)
    sum_b, send_b, rest = call(
        project_kernel,
        [sums[0], shape(3 * rows, kv_wide, jnp.bfloat16), shape(rows, kv_wide, jnp.bfloat16)],
        2 * kv_flops,
        8 * rows * half,
    )(near_b, near_b_s, far_a, far_a_s, key, value)
    early_b = swap(send_b, "ctx", 1)
    before = call(
        query_first_kernel,
        shape(2 * rows, wide, jnp.float32),
        4 * rows * half * wide,
        4 * rows * half,
        in_specs=[vmem] * 2 + [anywhere, vmem],
    )(near_b, near_b_s, early_a, w_near)

    far_c = swap(passed([x_far], before)[0], "tp", 2)
    parts = split_columns(half, 2)
    far_b, *pieces = passed(
        [far_b] * (len(parts) + 1), before, early_b, ranges=[(0, half), *parts]
    )
    pieces = [swap(piece, "tp", 1) for piece in pieces]
    far_sum_b = call(
        project_more_kernel,
        shape(3 * rows, kv_wide, jnp.bfloat16),
        kv_flops,
        4 * rows * half,
    )(rest, far_b, key, value, *pieces)
    more_b = swap(far_sum_b, "ctx", 1)
    parts = split_columns(half, 3)
    pieces = passed([far_c] * len(parts), far_sum_b, ranges=parts)
    pieces = [swap(piece, "tp", 1) for piece in pieces]
    q_last = call(
        query_last_kernel,
        shape(2 * rows, wide, jnp.bfloat16),
        4 * rows * half * wide,
        8 * rows * half,
    )(far_c, w_far, before, cosine, sine, *pieces)

    kv_shape = shape(4 * rows, kv_wide, jnp.bfloat16)
    done = call(finish_kernel, kv_shape, 1 << 24, 1 << 20)(
        send_b, far_sum_b, early_a, early_b, cosine, sine
    )
    attended = call(
        functools.partial(attend_kernel, group),
        shape(4 * rows, wide, jnp.bfloat16),
        8 * rows * 8 * rows * wide,
        1 << 20,
        scratch_shapes=[pltpu.VMEM((8 * rows, kv_wide), jnp.bfloat16)],
    )(q_first, q_last, done, sum_a, sum_b, early_b, more_b, cosine, sine, allowed)

    w_out = in_vmem(w_out)
    out, first = jnp.zeros((rows, w_out.shape[1]), jnp.bfloat16), 0
    sums = project_out(attended, w_out, 0, 1) + project_out(attended, w_out, 1, OUT_CHUNKS - 1)
    for stay, leave in sums:
        stay = stay + swap(leave, "tp", 1).astype(jnp.float32)
        arrived = swap(stay[rows:].astype(jnp.bfloat16), "tp", 2)
        part = from_behind(mix(stay[:rows], arrived), "pipe", 1)
        out = lax.dynamic_update_slice(out, part, (0, first))
        first += part.shape[1]
    return out[None]


def doc_index(positions, lengths):
    doc_ends = jnp.cumsum(lengths)
    return jnp.sum((positions[:, None] >= doc_ends[None, :]).astype(jnp.int32), axis=1)


def norm_rotate(entries, positions, head_count, head_width):
    row_count = entries.shape[0]
    shaped = entries.reshape(row_count, head_count, head_width)
    shaped = shaped * lax.rsqrt(jnp.mean(shaped * shaped, axis=-1, keepdims=True) + NORM_EPS)
    half_width = head_width // 2
    frequencies = jnp.power(
        ROPE_BASE, -(jnp.arange(half_width, dtype=jnp.float32) * 2.0 / head_width)
    )
    angles = positions.astype(jnp.float32)[:, None] * frequencies[None, :]
    cosine = jnp.cos(angles)[:, None, :]
    sine_part = jnp.sin(angles)[:, None, :]
    first_half = shaped[..., :half_width]
    second = shaped[..., half_width:]
    turned = jnp.concatenate(
        [first_half * cosine - second * sine_part, second * cosine + first_half * sine_part],
        axis=-1,
    )
    return turned.reshape(row_count, head_count * head_width)


def attend(queries, q_pos, q_doc, key_rows, value_rows, k_pos, k_doc):
    score_scale = 1.0 / HD**0.5
    scores = (
        jnp.einsum("tkgd,nkd->kgtn", queries, key_rows, preferred_element_type=jnp.float32)
        * score_scale
    )
    allowed = (
        (k_pos[None, :] <= q_pos[:, None])
        & (k_doc[None, :] == q_doc[:, None])
        & (k_pos[None, :] // SPAN == q_pos[:, None] // SPAN)
    )
    weights = jnp.where(allowed[None, None], jnp.exp(scores), 0.0).astype(jnp.bfloat16)
    numerator = jnp.einsum(
        "kgtn,nkd->tkgd", weights, value_rows, preferred_element_type=jnp.float32
    )
    denominator = jnp.sum(weights.astype(jnp.float32), axis=-1)
    return (numerator, denominator)


def on_any(inputs, doc_lengths, w_query, w_key, w_value, w_out):
    tok_rows = lax.all_gather(inputs[0], "tp", axis=0, tiled=True)
    block_rows = tok_rows.shape[0]
    q_heads = w_query.shape[2] // HD
    kv_heads = w_key.shape[2] // HD
    group_size = q_heads // kv_heads
    ctx_rank = lax.axis_index("ctx")
    positions = ctx_rank * block_rows + jnp.arange(block_rows, dtype=jnp.int32)
    lengths = doc_lengths[0]
    own_docs = doc_index(positions, lengths)
    queries = jnp.dot(tok_rows, w_query[0], preferred_element_type=jnp.float32)
    stacked_weights = jnp.stack([w_key[0], w_value[0]])
    key_value = jnp.einsum(
        "td,sdc->stc",
        tok_rows,
        lax.all_gather(stacked_weights, "ctx", axis=1, tiled=True),
        preferred_element_type=jnp.float32,
    )
    keys_float = key_value[0]
    values_float = key_value[1]
    q_round = (
        norm_rotate(queries, positions, q_heads, HD)
        .astype(jnp.bfloat16)
        .reshape(block_rows, kv_heads, group_size, HD)
    )
    k_round = norm_rotate(keys_float, positions, kv_heads, HD).astype(jnp.bfloat16)
    v_round = values_float.astype(jnp.bfloat16)
    key_value_pair = jnp.stack([k_round, v_round])
    shard_piece = lax.all_gather(key_value_pair, "ctx", axis=1, tiled=True)
    row_count = shard_piece.shape[1]
    k_pos = jnp.arange(row_count, dtype=jnp.int32)
    k_doc = doc_index(k_pos, lengths)
    key_rows = shard_piece[0].reshape(row_count, kv_heads, HD)
    value_rows = shard_piece[1].reshape(row_count, kv_heads, HD)
    numerator, denominator = attend(
        q_round, positions, own_docs, key_rows, value_rows, k_pos, k_doc
    )
    attended = (
        (numerator / jnp.transpose(denominator, (2, 0, 1))[..., None])
        .astype(jnp.bfloat16)
        .reshape(block_rows, q_heads * HD)
    )
    mixed = lax.psum_scatter(
        jnp.dot(attended, w_out[0], preferred_element_type=jnp.float32).astype(jnp.bfloat16),
        "tp",
        scatter_dimension=0,
        tiled=True,
    )
    return from_behind(mixed, "pipe", 1)[None]


def solution(mesh):
    in_specs = (
        P("pipe", ("ctx", "tp"), None),
        P("pipe", None),
        P("pipe", None, "tp"),
        P("pipe", "ctx", "tp"),
        P("pipe", "ctx", "tp"),
        P("pipe", "tp", None),
    )
    out_specs = P("pipe", ("ctx", "tp"), None)
    paired = mesh.shape["ctx"] == 2 and mesh.shape["tp"] == 4
    return jax.shard_map(
        on_four_by_two if paired else on_any,
        mesh=mesh,
        in_specs=in_specs,
        out_specs=out_specs,
        check_vma=False,
    )
```

```python
import functools
import math

import jax
import jax.numpy as jnp
from jax import lax
from jax.experimental import pallas as pl
from jax.experimental.pallas import tpu as pltpu
from jax.sharding import PartitionSpec as P

HD = 128
SPAN = 1024
ROPE_BASE = 500000.0
NORM_EPS = 1e-06
MASKED = -1e30
OUT_CHUNKS = 5
MIB = 1 << 20
VMEM_MIB = 16


def from_behind(value, axis, steps):
    count = lax.axis_size(axis)
    pairs = [(source, (source + steps) % count) for source in range(count)]
    return lax.ppermute(value, axis, pairs)


def swap(value, axis, bit):
    count = lax.axis_size(axis)
    return lax.ppermute(value, axis, [(source, source ^ bit) for source in range(count)])


def norm_rotate_head(head, cosine, sine):
    head = head * lax.rsqrt(jnp.mean(head * head, axis=-1, keepdims=True) + NORM_EPS)
    return head * cosine + pltpu.roll(head, HD // 2, 1) * sine


def shape(rows, columns, dtype):
    return jax.ShapeDtypeStruct((rows, columns), dtype)


def in_vmem(value):
    return pltpu.with_memory_space_constraint(value, pltpu.VMEM)


def in_hbm(value):
    return pltpu.with_memory_space_constraint(value, pltpu.HBM)


def call(kernel, out_shape, flops, moved, **given):
    return pl.pallas_call(
        kernel,
        out_shape=out_shape,
        compiler_params=pltpu.CompilerParams(vmem_limit_bytes=VMEM_MIB * MIB),
        cost_estimate=pl.CostEstimate(flops=flops, bytes_accessed=moved, transcendentals=0),
        **given,
    )


def split_kernel(value, near, far, sems):
    wide = near.shape[1]
    at = pl.multiple_of(lax.axis_index("ctx") * wide, wide)
    near_copy = pltpu.make_async_copy(value.at[:, pl.ds(at, wide)], near, sems.at[0])
    far_copy = pltpu.make_async_copy(value.at[:, pl.ds(wide - at, wide)], far, sems.at[1])
    near_copy.start()
    far_copy.start()
    near_copy.wait()
    far_copy.wait()


def pass_kernel(ranges, *refs):
    count = len(ranges)
    for value, out, (start, stop) in zip(refs[:count], refs[-count:], ranges):
        out[...] = value[:, start:stop]


def passed(values, *tokens, ranges=None):
    vmem, anywhere = pl.BlockSpec(memory_space=pltpu.VMEM), pl.BlockSpec(memory_space=pl.ANY)
    ranges = ranges or [(0, value.shape[1]) for value in values]
    return call(
        functools.partial(pass_kernel, ranges),
        [
            shape(value.shape[0], stop - start, value.dtype)
            for value, (start, stop) in zip(values, ranges)
        ],
        0,
        1 << 20,
        in_specs=[vmem] * len(values) + [anywhere] * len(tokens),
    )(*[in_vmem(value) for value in values], *tokens)


def split_columns(wide, count):
    tiles = wide // HD
    cuts = [tiles * at // count * HD for at in range(count + 1)]
    return list(zip(cuts[:-1], cuts[1:]))


def fill_tables(rows, block_rows, lengths, cosine, sine, allowed):
    start, index = lax.axis_index("ctx") * block_rows, lax.axis_index("tp")
    offsets = [start + shift + rows * (index ^ flip) for shift in (-block_rows, 0) for flip in range(4)]
    lane = lax.broadcasted_iota(jnp.int32, (1, HD), 1)
    power = (lane % (HD // 2)).astype(jnp.float32) * (2.0 / HD)
    frequency = jnp.exp(power * -math.log(ROPE_BASE))
    sign = jnp.where(lane < HD // 2, -1.0, 1.0)
    step = lax.broadcasted_iota(jnp.int32, (rows, HD), 0).astype(jnp.float32) * frequency
    step_cosine, step_sine = jnp.cos(step), jnp.sin(step)
    order = lax.broadcasted_iota(jnp.int32, (8, HD), 0)
    origin = jnp.zeros((8, HD), jnp.int32)
    for at, offset in enumerate(offsets):
        origin = jnp.where(order == at, offset, origin)
    origin = origin.astype(jnp.float32) * frequency
    origin_cosine, origin_sine = jnp.cos(origin), jnp.sin(origin)
    for at in range(8):
        part = pl.ds(at * rows, rows)
        far_cosine, far_sine = origin_cosine[at : at + 1, :], origin_sine[at : at + 1, :]
        cosine[part, :] = step_cosine * far_cosine - step_sine * far_sine
        sine[part, :] = (step_sine * far_cosine + step_cosine * far_sine) * sign

    row = lax.broadcasted_iota(jnp.int32, (rows, HD), 0)
    column = lax.broadcasted_iota(jnp.int32, (1, HD), 1)
    ends, end = [], 0
    for doc in range(lengths.shape[1]):
        end = end + lengths[0, doc]
        ends.append(end)
    for at in range(4):
        q_pos = row + offsets[4 + at]
        first = q_pos // SPAN * SPAN
        for end in ends:
            first = jnp.where(end <= q_pos, jnp.maximum(first, end), first)
        for to in range(0, 8 * rows, HD):
            k_pos = column + offsets[to // rows]
            for half in range(1, HD // rows):
                other = column + (offsets[to // rows + half] - half * rows)
                k_pos = jnp.where(column >= half * rows, other, k_pos)
            inside = (k_pos >= first) & (k_pos <= q_pos)
            allowed[at * rows : (at + 1) * rows, to : to + HD] = jnp.where(inside, 0.0, MASKED)


def stacked(pieces):
    return jnp.concatenate([piece[...] for piece in pieces], axis=0)


def stacked_parts(own, parts):
    other = jnp.concatenate([part[...] for part in parts], axis=1) if len(parts) > 1 else parts[0][...]
    return jnp.concatenate([own[...], other], axis=0)


def put(total, to, *outs):
    for out in outs:
        out[:, to] = total.astype(out.dtype)


def own_kernel(block_rows, lengths, n0, f0, other, w_key, w_value, w, *refs):
    own_sum, own_send, query, key, value, w_near, w_far, cosine, sine, allowed, sems = refs
    piece, depth = n0.shape
    ctx = lax.axis_index("ctx")
    near_rows = w.at[pl.ds(pl.multiple_of(ctx * depth, depth), depth)]
    far_rows = w.at[pl.ds(pl.multiple_of((1 - ctx) * depth, depth), depth)]
    pairs = ((w_key, key), (w_value, value), (near_rows, w_near), (far_rows, w_far))
    copies = [pltpu.make_async_copy(*pair, sems.at[i]) for i, pair in enumerate(pairs)]
    for copy in copies:
        copy.start()
    fill_tables(piece, block_rows, lengths, cosine, sine, allowed)
    at = pl.multiple_of(ctx * depth, depth)
    near = jnp.concatenate([n0[...], other[:, pl.ds(at, depth)]], axis=0)
    far = jnp.concatenate([f0[...], other[:, pl.ds(depth - at, depth)]], axis=0)
    wide = key.shape[1]
    for index, weight in enumerate((key, value)):
        copies[index].wait()
        total = jnp.dot(near, weight[...], preferred_element_type=jnp.float32)
        put(total, slice(index * wide, (index + 1) * wide), own_sum, own_send)
    block = 2 * HD
    copies[2].wait()
    columns = range(0, w.shape[1], block)
    first = [
        jnp.dot(near, w_near[:, at : at + block], preferred_element_type=jnp.float32)
        for at in columns
    ]
    copies[3].wait()
    turn = pl.ds(4 * piece, 2 * piece)
    for at, total in zip(columns, first):
        total += jnp.dot(far, w_far[:, at : at + block], preferred_element_type=jnp.float32)
        for head in range(0, block, HD):
            turned = norm_rotate_head(total[:, head : head + HD], cosine[turn, :], sine[turn, :])
            query[:, at + head : at + head + HD] = turned.astype(query.dtype)


def project_kernel(n0, n1, f0, f1, key, value, own_sum, send, rest):
    rows = stacked((n0, n1, f0, f1))
    whole, ready, wide = own_sum.shape[0], send.shape[0], key.shape[1]
    for index, weight in enumerate((key, value)):
        to = slice(index * wide, (index + 1) * wide)
        total = jnp.dot(rows, weight[...], preferred_element_type=jnp.float32)
        put(total[:whole], to, own_sum)
        put(total[:ready], to, send)
        put(total[ready:], to, rest)


def query_first_kernel(n0, n1, _, w, out):
    out[...] = jnp.dot(stacked((n0, n1)), w[...], preferred_element_type=jnp.float32)


def project_more_kernel(before, x0, w0, w1, *refs):
    rows, out = stacked_parts(x0, refs[:-1]), refs[-1]
    ready, wide = before.shape[0], w0.shape[1]
    out[:ready, :] = before[...]
    for index, w in enumerate((w0, w1)):
        total = jnp.dot(rows, w[...], preferred_element_type=jnp.float32)
        out[ready:, index * wide : (index + 1) * wide] = total.astype(out.dtype)


def query_last_kernel(f0, w, before, cosine, sine, *refs):
    rows, out = stacked_parts(f0, refs[:-1]), refs[-1]
    block = 2 * HD
    turn = pl.ds(3 * rows.shape[0], rows.shape[0])
    for at in range(0, w.shape[1], block):
        total = jnp.dot(rows, w[:, at : at + block], preferred_element_type=jnp.float32)
        total = total + before[:, at : at + block]
        for head in range(0, block, HD):
            query = norm_rotate_head(total[:, head : head + HD], cosine[turn, :], sine[turn, :])
            out[:, at + head : at + head + HD] = query.astype(out.dtype)


def finish(total, cosine, sine, out, at):
    rows, wide = total.shape
    keys = wide // 2
    part = pl.ds(at, rows)
    for head in range(0, keys, HD):
        key = norm_rotate_head(total[:, head : head + HD], cosine[part, :], sine[part, :])
        out[part, head : head + HD] = key.astype(out.dtype)
    out[part, keys:] = total[:, keys:].astype(out.dtype)


def finish_kernel(send, far, early_a, early_b, cosine, sine, out):
    rows = early_a.shape[0]
    early = jnp.concatenate([early_a[...], early_b[:rows, :]], axis=0)
    far = jnp.concatenate([send[rows:, :], far[...]], axis=0)
    finish(early.astype(jnp.float32) + far.astype(jnp.float32), cosine, sine, out, 0)


def attend_kernel(group, q_first, q_last, done, sum_a, sum_b, more_a, more_b, cosine, sine, allowed, out, kv):
    rows = 2 * q_first.shape[0]
    ready = done.shape[0]
    kv[:ready, :] = done[...]
    half = sum_a.shape[0]
    total = jnp.concatenate([sum_a[...], sum_b[...]], axis=0)
    more = jnp.concatenate([more_a[half:, :], more_b[...]], axis=0)
    finish(total + more.astype(jnp.float32), cosine, sine, kv, ready)
    keys = kv.shape[1] // 2
    bias = jnp.concatenate([allowed[...]] * group, axis=0)
    ones = jnp.ones((kv.shape[0], HD), kv.dtype)
    for head in range(0, keys, HD):
        key = kv[:, head : head + HD]
        value = kv[:, keys + head : keys + head + HD]
        at = head * group
        columns = [slice(at + g * HD, at + (g + 1) * HD) for g in range(group)]
        query = jnp.concatenate([q[:, c] for c in columns for q in (q_first, q_last)], 0)
        scores = lax.dot_general(
            query, key, (((1,), (1,)), ((), ())), preferred_element_type=jnp.float32
        )
        weights = jnp.exp(scores * (1.0 / HD**0.5) + bias).astype(jnp.bfloat16)
        value = jnp.concatenate([value, ones], axis=1)
        mixed = jnp.dot(weights, value, preferred_element_type=jnp.float32)
        mixed = (mixed[:, :HD] / mixed[:, HD:]).astype(out.dtype)
        for g, c in enumerate(columns):
            out[:, c] = mixed[g * rows : (g + 1) * rows, :]


def out_kernel(first, attended, w, *refs):
    stays, leaves = refs[::2], refs[1::2]
    half, wide = stays[0].shape
    rows = half // 2
    block = 2 * HD
    for chunk, (stay, leave) in enumerate(zip(stays, leaves)):
        for at in range(0, wide, block):
            part = pl.ds((first + chunk) * wide + at, block)
            total = jnp.dot(attended[...], w[:, part], preferred_element_type=jnp.float32)
            for to, (index, out) in enumerate(((0, stay), (1, leave), (2, stay), (3, leave))):
                piece = total[index * rows : (index + 1) * rows].astype(out.dtype)
                out[to // 2 * rows : to // 2 * rows + rows, at : at + block] = piece


def project_out(attended, w, first, chunks):
    rows, depth = attended.shape
    wide = w.shape[1] // OUT_CHUNKS
    pair = [shape(rows // 2, wide, jnp.float32), shape(rows // 2, wide, jnp.bfloat16)]
    outs = call(
        functools.partial(out_kernel, first),
        pair * chunks,
        2 * rows * depth * wide * chunks,
        2 * rows * depth,
    )(attended, w)
    return list(zip(outs[::2], outs[1::2]))


def mix_kernel(stay, arrived, out):
    out[...] = (stay[...] + arrived[...].astype(jnp.float32)).astype(out.dtype)


def mix(stay, arrived):
    return call(mix_kernel, shape(*arrived.shape, arrived.dtype), 0, 1 << 20)(stay, arrived)


def on_four_by_two(inputs, doc_lengths, w_query, w_key, w_value, w_out):
    own = inputs[0]
    w_query, w_key, w_value, w_out = w_query[0], w_key[0], w_value[0], w_out[0]
    rows = own.shape[0]
    half = w_key.shape[0]
    group = w_query.shape[1] // w_key.shape[1]
    block_rows = rows * lax.axis_size("tp")

    smem, vmem = pl.BlockSpec(memory_space=pltpu.SMEM), pl.BlockSpec(memory_space=pltpu.VMEM)
    anywhere = pl.BlockSpec(memory_space=pl.ANY)

    x_near, x_far = call(
        split_kernel,
        [shape(rows, half, own.dtype)] * 2,
        0,
        1 << 20,
        in_specs=[anywhere],
        scratch_shapes=[pltpu.SemaphoreType.DMA((2,))],
    )(in_hbm(own))
    far_a = swap(x_far, "ctx", 1)
    near_b = swap(x_near, "tp", 2)
    own_s = swap(own, "tp", 1)

    wide = w_query.shape[1]
    kv_wide = 2 * w_key.shape[1]
    kv_flops = 4 * rows * half * kv_wide
    sums = [shape(2 * rows, kv_wide, jnp.float32), shape(2 * rows, kv_wide, jnp.bfloat16)]
    sum_a, send_a, q_first, key, value, w_near, w_far, cosine, sine, allowed = call(
        functools.partial(own_kernel, block_rows),
        [
            *sums,
            shape(2 * rows, wide, jnp.bfloat16),
            *[shape(*w_key.shape, jnp.bfloat16)] * 2,
            *[shape(half, wide, jnp.bfloat16)] * 2,
            *[shape(8 * rows, HD, jnp.float32)] * 2,
            shape(4 * rows, 8 * rows, jnp.float32),
        ],
        kv_flops + 8 * rows * half * wide,
        8 * rows * half,
        in_specs=[smem] + [vmem] * 3 + [anywhere] * 3,
        scratch_shapes=[pltpu.SemaphoreType.DMA((4,))],
    )(
        in_hbm(doc_lengths),
        *(x_near, x_far, own_s),
        *(in_hbm(w_key), in_hbm(w_value), in_hbm(w_query)),
    )
    key, value, w_near, w_far = in_vmem(key), in_vmem(value), in_vmem(w_near), in_vmem(w_far)

    far_a, near_b, send_a = passed([far_a, near_b, send_a])
    far_b = swap(far_a, "tp", 2)
    early_a = swap(send_a, "ctx", 1)
    near_b_s = swap(near_b, "tp", 1)
    far_a_s = swap(far_a, "tp", 1)
    sum_b, send_b, rest = call(
        project_kernel,
        [sums[0], shape(3 * rows, kv_wide, jnp.bfloat16), shape(rows, kv_wide, jnp.bfloat16)],
        2 * kv_flops,
        8 * rows * half,
    )(near_b, near_b_s, far_a, far_a_s, key, value)
    early_b = swap(send_b, "ctx", 1)
    before = call(
        query_first_kernel,
        shape(2 * rows, wide, jnp.float32),
        4 * rows * half * wide,
        4 * rows * half,
        in_specs=[vmem] * 2 + [anywhere, vmem],
    )(near_b, near_b_s, early_a, w_near)

    far_c = swap(passed([x_far], before)[0], "tp", 2)
    parts = split_columns(half, 2)
    far_b, *pieces = passed(
        [far_b] * (len(parts) + 1), before, early_b, ranges=[(0, half), *parts]
    )
    pieces = [swap(piece, "tp", 1) for piece in pieces]
    far_sum_b = call(
        project_more_kernel,
        shape(3 * rows, kv_wide, jnp.bfloat16),
        kv_flops,
        4 * rows * half,
    )(rest, far_b, key, value, *pieces)
    more_b = swap(far_sum_b, "ctx", 1)
    parts = split_columns(half, 3)
    pieces = passed([far_c] * len(parts), far_sum_b, ranges=parts)
    pieces = [swap(piece, "tp", 1) for piece in pieces]
    q_last = call(
        query_last_kernel,
        shape(2 * rows, wide, jnp.bfloat16),
        4 * rows * half * wide,
        8 * rows * half,
    )(far_c, w_far, before, cosine, sine, *pieces)

    kv_shape = shape(4 * rows, kv_wide, jnp.bfloat16)
    done = call(finish_kernel, kv_shape, 1 << 24, 1 << 20)(
        send_b, far_sum_b, early_a, early_b, cosine, sine
    )
    attended = call(
        functools.partial(attend_kernel, group),
        shape(4 * rows, wide, jnp.bfloat16),
        8 * rows * 8 * rows * wide,
        1 << 20,
        scratch_shapes=[pltpu.VMEM((8 * rows, kv_wide), jnp.bfloat16)],
    )(q_first, q_last, done, sum_a, sum_b, early_b, more_b, cosine, sine, allowed)

    w_out = in_vmem(w_out)
    out, first = jnp.zeros((rows, w_out.shape[1]), jnp.bfloat16), 0
    sums = project_out(attended, w_out, 0, 1) + project_out(attended, w_out, 1, OUT_CHUNKS - 1)
    for stay, leave in sums:
        stay = stay + swap(leave, "tp", 1).astype(jnp.float32)
        arrived = swap(stay[rows:].astype(jnp.bfloat16), "tp", 2)
        part = from_behind(mix(stay[:rows], arrived), "pipe", 1)
        out = lax.dynamic_update_slice(out, part, (0, first))
        first += part.shape[1]
    return out[None]


def doc_index(positions, lengths):
    doc_ends = jnp.cumsum(lengths)
    return jnp.sum((positions[:, None] >= doc_ends[None, :]).astype(jnp.int32), axis=1)


def norm_rotate(entries, positions, head_count, head_width):
    row_count = entries.shape[0]
    shaped = entries.reshape(row_count, head_count, head_width)
    shaped = shaped * lax.rsqrt(jnp.mean(shaped * shaped, axis=-1, keepdims=True) + NORM_EPS)
    half_width = head_width // 2
    frequencies = jnp.power(
        ROPE_BASE, -(jnp.arange(half_width, dtype=jnp.float32) * 2.0 / head_width)
    )
    angles = positions.astype(jnp.float32)[:, None] * frequencies[None, :]
    cosine = jnp.cos(angles)[:, None, :]
    sine_part = jnp.sin(angles)[:, None, :]
    first_half = shaped[..., :half_width]
    second = shaped[..., half_width:]
    turned = jnp.concatenate(
        [first_half * cosine - second * sine_part, second * cosine + first_half * sine_part],
        axis=-1,
    )
    return turned.reshape(row_count, head_count * head_width)


def attend(queries, q_pos, q_doc, key_rows, value_rows, k_pos, k_doc):
    score_scale = 1.0 / HD**0.5
    scores = (
        jnp.einsum("tkgd,nkd->kgtn", queries, key_rows, preferred_element_type=jnp.float32)
        * score_scale
    )
    allowed = (
        (k_pos[None, :] <= q_pos[:, None])
        & (k_doc[None, :] == q_doc[:, None])
        & (k_pos[None, :] // SPAN == q_pos[:, None] // SPAN)
    )
    weights = jnp.where(allowed[None, None], jnp.exp(scores), 0.0).astype(jnp.bfloat16)
    numerator = jnp.einsum(
        "kgtn,nkd->tkgd", weights, value_rows, preferred_element_type=jnp.float32
    )
    denominator = jnp.sum(weights.astype(jnp.float32), axis=-1)
    return (numerator, denominator)


def on_any(inputs, doc_lengths, w_query, w_key, w_value, w_out):
    tok_rows = lax.all_gather(inputs[0], "tp", axis=0, tiled=True)
    block_rows = tok_rows.shape[0]
    q_heads = w_query.shape[2] // HD
    kv_heads = w_key.shape[2] // HD
    group_size = q_heads // kv_heads
    ctx_rank = lax.axis_index("ctx")
    positions = ctx_rank * block_rows + jnp.arange(block_rows, dtype=jnp.int32)
    lengths = doc_lengths[0]
    own_docs = doc_index(positions, lengths)
    queries = jnp.dot(tok_rows, w_query[0], preferred_element_type=jnp.float32)
    stacked_weights = jnp.stack([w_key[0], w_value[0]])
    key_value = jnp.einsum(
        "td,sdc->stc",
        tok_rows,
        lax.all_gather(stacked_weights, "ctx", axis=1, tiled=True),
        preferred_element_type=jnp.float32,
    )
    keys_float = key_value[0]
    values_float = key_value[1]
    q_round = (
        norm_rotate(queries, positions, q_heads, HD)
        .astype(jnp.bfloat16)
        .reshape(block_rows, kv_heads, group_size, HD)
    )
    k_round = norm_rotate(keys_float, positions, kv_heads, HD).astype(jnp.bfloat16)
    v_round = values_float.astype(jnp.bfloat16)
    key_value_pair = jnp.stack([k_round, v_round])
    shard_piece = lax.all_gather(key_value_pair, "ctx", axis=1, tiled=True)
    row_count = shard_piece.shape[1]
    k_pos = jnp.arange(row_count, dtype=jnp.int32)
    k_doc = doc_index(k_pos, lengths)
    key_rows = shard_piece[0].reshape(row_count, kv_heads, HD)
    value_rows = shard_piece[1].reshape(row_count, kv_heads, HD)
    numerator, denominator = attend(
        q_round, positions, own_docs, key_rows, value_rows, k_pos, k_doc
    )
    attended = (
        (numerator / jnp.transpose(denominator, (2, 0, 1))[..., None])
        .astype(jnp.bfloat16)
        .reshape(block_rows, q_heads * HD)
    )
    mixed = lax.psum_scatter(
        jnp.dot(attended, w_out[0], preferred_element_type=jnp.float32).astype(jnp.bfloat16),
        "tp",
        scatter_dimension=0,
        tiled=True,
    )
    return from_behind(mixed, "pipe", 1)[None]


def solution(mesh):
    in_specs = (
        P("pipe", ("ctx", "tp"), None),
        P("pipe", None),
        P("pipe", None, "tp"),
        P("pipe", "ctx", "tp"),
        P("pipe", "ctx", "tp"),
        P("pipe", "tp", None),
    )
    out_specs = P("pipe", ("ctx", "tp"), None)
    paired = mesh.shape["ctx"] == 2 and mesh.shape["tp"] == 4
    return jax.shard_map(
        on_four_by_two if paired else on_any,
        mesh=mesh,
        in_specs=in_specs,
        out_specs=out_specs,
        check_vma=False,
    )
```
